32 devices in a mesh: prefix: 4 (over z), group: 4 (over y, core), tensor: 2 (over x).
Axes of the slice: x: 2, y: 2, z: 4, core: 2. Of those that a mesh axis runs over, the one named last changes fastest.
Arguments:
- resp_query: bfloat16 [512, 8, 32, 128], P('prefix', 'group', 'tensor'), may hold values from -6 to 6
- response_key: bfloat16 [512, 8, 4, 128], P('prefix', 'group', 'tensor'), may hold values from -6 to 6
- response_value: bfloat16 [512, 8, 4, 128], P('prefix', 'group', 'tensor'), may hold values from -6 to 6
- resp_cotangent: bfloat16 [512, 8, 32, 128], P('prefix', 'group', 'tensor'), may hold values from -300 to 300
- prompt_key: bfloat16 [256, 4, 128], P('prefix', 'tensor'), may hold values from -6.2 to 6.2
- prompt_value_rows: bfloat16 [256, 4, 128], P('prefix', 'tensor'), may hold values from -6 to 6
- key_matrix: bfloat16 [5120, 512], P(None, 'tensor'), may hold values from -0.078125 to 0.078125
- value_matrix: bfloat16 [5120, 512], P(None, 'tensor'), may hold values from -0.078125 to 0.078125
- resp_lengths: int32 [8], replicated, may hold values from 128 to 512, as said below
Outputs:
- resp_query_grad: bfloat16 [512, 8, 32, 128], P('prefix', 'group', 'tensor')
- resp_key_grad: bfloat16 [512, 8, 4, 128], P('prefix', 'group', 'tensor')
- resp_value_grad: bfloat16 [512, 8, 4, 128], P('prefix', 'group', 'tensor')
- prompt_input_grad: bfloat16 [256, 5120], P('prefix', 'tensor')
The draws below stay inside these ranges and needn't reach their ends.
Inputs may be any that keep to these rules, and one draw needn't show every extreme that they name: `resp_lengths`: some response has all 512 tokens and another 512 // 4 in every draw.
All inputs are finite; a program needn't handle non-finite values.
Results may differ from the reference program's by a relative error of at most 0.0058.
Values may be sent and summed in bfloat16 or wider, within the bound.
A program may use at most 128 MiB of HBM per device.

```python
import math
import jax
import jax.numpy as jnp
from jax import lax

MODEL_WIDTH = 5120
HEAD_SIZE = 128
QUERY_HEAD_COUNT = 32
KEY_VALUE_HEADS = 4
PROMPT_LENGTH = 256
RESPONSE_LENGTH = 512
RESPONSE_COUNT = 8


def draw_resp_query(key, part):
    key = jax.random.fold_in(key, 11)
    key_first = jax.random.fold_in(key, 0)
    value_rows = jnp.clip(jax.random.normal(key_first, (RESPONSE_LENGTH, RESPONSE_COUNT, QUERY_HEAD_COUNT, HEAD_SIZE), jnp.float32), -6.0, 6.0)
    return value_rows.astype(jnp.bfloat16)


def draw_prompt_key(key, part):
    key = jax.random.fold_in(key, 23)
    key_first = jax.random.fold_in(key, 0)
    value_rows = jnp.clip(jax.random.normal(key_first, (PROMPT_LENGTH, KEY_VALUE_HEADS, HEAD_SIZE), jnp.float32), -6.0, 6.0)
    return value_rows.astype(jnp.bfloat16)


def draw_resp_lengths(key, part):
    key = jax.random.fold_in(key, 37)
    key_first, key_two, key_three = jax.random.split(key, 3)
    lengths = jax.random.randint(key_first, (RESPONSE_COUNT,), RESPONSE_LENGTH // 4, RESPONSE_LENGTH + 1)
    full_index = jax.random.randint(key_two, (), 0, RESPONSE_COUNT)
    short_index = (full_index + 1 + jax.random.randint(key_three, (), 0, RESPONSE_COUNT - 1)) % RESPONSE_COUNT
    row_ids = jnp.arange(RESPONSE_COUNT)
    lengths = jnp.where(row_ids == full_index, RESPONSE_LENGTH, lengths)
    lengths = jnp.where(row_ids == short_index, RESPONSE_LENGTH // 4, lengths)
    return lengths.astype(jnp.int32)


def shard_levels(stream_key, shape, shards, low, largest):
    gain, own = 1.0, jax.random.fold_in(stream_key, 6)
    for dim, shards_of in shards:
        draws = jnp.exp(jax.random.uniform(jax.random.fold_in(own, dim), (shards_of,), jnp.float32, low / len(shards), largest / len(shards)))
        gain = gain * jnp.repeat(draws, shape[dim] // shards_of).reshape([-1 if axis == dim else 1 for axis in range(len(shape))])
    return gain


def bell_draw(rng, dims, deviation, limit, cuts=(), kind=jnp.bfloat16):
    entries = deviation * jax.random.normal(rng, dims, jnp.float32)
    if cuts:
        entries = entries * shard_levels(rng, dims, cuts, -0.22, 0.18)
    return jnp.clip(entries, -limit, limit).astype(kind)


def setup_inputs(seed: int = 0) -> dict:
    seeds = jax.random.split(jax.random.key(seed), 10)
    resp_query = draw_resp_query(jax.random.fold_in(seeds[9], 71), 0)
    response_key = bell_draw(seeds[1], (RESPONSE_LENGTH, RESPONSE_COUNT, KEY_VALUE_HEADS, HEAD_SIZE), 1.0, 6.0, ((0, 4), (1, 4), (2, 2)))
    response_value = bell_draw(seeds[2], (RESPONSE_LENGTH, RESPONSE_COUNT, KEY_VALUE_HEADS, HEAD_SIZE), 1.0, 6.0, ((0, 4), (1, 4), (2, 2)))
    resp_cotangent = bell_draw(seeds[3], (RESPONSE_LENGTH, RESPONSE_COUNT, QUERY_HEAD_COUNT, HEAD_SIZE), 50.0, 300.0, ((0, 4), (1, 4), (2, 2)))
    prompt_key = draw_prompt_key(jax.random.fold_in(seeds[9], 71), 0)
    prompt_value_rows = bell_draw(seeds[5], (PROMPT_LENGTH, KEY_VALUE_HEADS, HEAD_SIZE), 1.0, 6.0, ((0, 4), (1, 2)))
    key_matrix = bell_draw(seeds[6], (MODEL_WIDTH, KEY_VALUE_HEADS * HEAD_SIZE), MODEL_WIDTH ** -0.5, 0.078125, ((1, 2),))
    value_matrix = bell_draw(seeds[7], (MODEL_WIDTH, KEY_VALUE_HEADS * HEAD_SIZE), MODEL_WIDTH ** -0.5, 0.078125, ((1, 2),))
    resp_lengths = draw_resp_lengths(jax.random.fold_in(seeds[9], 71), 0)
    return dict(resp_query=resp_query, response_key=response_key, response_value=response_value, resp_cotangent=resp_cotangent, prompt_key=prompt_key, prompt_value_rows=prompt_value_rows, key_matrix=key_matrix, value_matrix=value_matrix, resp_lengths=resp_lengths)


masked_score = -1e+30

def reference(resp_query, response_key, response_value, resp_cotangent, prompt_key, prompt_value_rows, key_matrix, value_matrix, resp_lengths):
    group_factor = QUERY_HEAD_COUNT // KEY_VALUE_HEADS
    score_scale = 1.0 / math.sqrt(HEAD_SIZE)
    prompt_keys = prompt_key.astype(jnp.float32)
    prompt_values = prompt_value_rows.astype(jnp.float32)
    positions = jnp.arange(RESPONSE_LENGTH, dtype=jnp.int32)
    key_pos = jnp.arange(PROMPT_LENGTH + RESPONSE_LENGTH, dtype=jnp.int32) - PROMPT_LENGTH
    visible = key_pos[None, :] <= positions[:, None]

    def one_response(state, pieces):
        query_first, key_first, value_one, cot_one, length_one = pieces
        query_float = query_first.reshape(RESPONSE_LENGTH, KEY_VALUE_HEADS, group_factor, HEAD_SIZE).astype(jnp.float32)
        live_rows = positions < length_one
        cotangent_active = jnp.where(live_rows[:, None, None], cot_one, jnp.zeros_like(cot_one))
        cotangent_float = cotangent_active.reshape(RESPONSE_LENGTH, KEY_VALUE_HEADS, group_factor, HEAD_SIZE).astype(jnp.float32)
        keys_f = jnp.concatenate([prompt_keys, key_first.astype(jnp.float32)], axis=0)
        values_f = jnp.concatenate([prompt_values, value_one.astype(jnp.float32)], axis=0)
        scores = jnp.einsum('lkge,mke->kglm', query_float, keys_f) * score_scale
        scores = jnp.where(visible, scores, masked_score)
        row_max = lax.optimization_barrier(jnp.max(scores, axis=-1))
        log_total = row_max + jnp.log(lax.optimization_barrier(jnp.sum(jnp.exp(scores - row_max[..., None]), axis=-1)))
        probs = jnp.exp(scores - log_total[..., None])
        dprob = jnp.einsum('lkge,mke->kglm', cotangent_float, values_f)
        row_delta = lax.optimization_barrier(jnp.sum(probs * dprob, axis=-1))
        dscore_low = lax.optimization_barrier((probs * (dprob - row_delta[..., None])).astype(jnp.bfloat16))
        prob_low = lax.optimization_barrier(probs.astype(jnp.bfloat16))
        dscore_f = dscore_low.astype(jnp.float32)
        prob_f = prob_low.astype(jnp.float32)
        value_sum = jnp.einsum('kglm,lkge->mke', prob_f, cotangent_float)
        key_sum = jnp.einsum('kglm,lkge->mke', dscore_f, query_float) * score_scale
        query_grad = jnp.einsum('kglm,mke->lkge', dscore_f, keys_f) * score_scale
        state = (state[0] + key_sum[:PROMPT_LENGTH], state[1] + value_sum[:PROMPT_LENGTH])
        outputs = (query_grad.reshape(RESPONSE_LENGTH, QUERY_HEAD_COUNT, HEAD_SIZE).astype(jnp.bfloat16), key_sum[PROMPT_LENGTH:].astype(jnp.bfloat16), value_sum[PROMPT_LENGTH:].astype(jnp.bfloat16))
        return (state, outputs)
    initial_state = (jnp.zeros((PROMPT_LENGTH, KEY_VALUE_HEADS, HEAD_SIZE), jnp.float32), jnp.zeros((PROMPT_LENGTH, KEY_VALUE_HEADS, HEAD_SIZE), jnp.float32))
    pieces = (jnp.moveaxis(resp_query, 1, 0), jnp.moveaxis(response_key, 1, 0), jnp.moveaxis(response_value, 1, 0), jnp.moveaxis(resp_cotangent, 1, 0), resp_lengths)
    prompt_totals, outputs = lax.scan(one_response, initial_state, pieces)
    prompt_key_gradient = prompt_totals[0].astype(jnp.bfloat16).reshape(PROMPT_LENGTH, KEY_VALUE_HEADS * HEAD_SIZE)
    prompt_value_gradient = prompt_totals[1].astype(jnp.bfloat16).reshape(PROMPT_LENGTH, KEY_VALUE_HEADS * HEAD_SIZE)
    prompt_input_grad = (jnp.dot(prompt_key_gradient, key_matrix.T, preferred_element_type=jnp.float32) + jnp.dot(prompt_value_gradient, value_matrix.T, preferred_element_type=jnp.float32)).astype(jnp.bfloat16)
    resp_query_grad = jnp.moveaxis(outputs[0], 0, 1)
    resp_key_grad = jnp.moveaxis(outputs[1], 0, 1)
    resp_value_grad = jnp.moveaxis(outputs[2], 0, 1)
    return (resp_query_grad, resp_key_grad, resp_value_grad, prompt_input_grad)
```

```python
import functools
import math

import jax
import jax.numpy as jnp
from jax import lax
from jax.experimental import pallas as pl
from jax.experimental.pallas import tpu as pltpu
from jax.sharding import PartitionSpec as P

MESH = pl.DeviceIdType.MESH
masked_score = -1e30
log2_e = math.log2(math.e)


def dot_nt(a, b):
    return lax.dot_general(a, b, (((1,), (1,)), ((), ())), preferred_element_type=jnp.float32)


def dot_nn(a, b):
    return lax.dot_general(a, b, (((1,), (0,)), ((), ())), preferred_element_type=jnp.float32)


def kernel(
    sizes,
    len_ref,
    kv_ref,
    pr_ref,
    q_ref,
    cot_ref,
    km_ref,
    vm_ref,
    dq_ref,
    dkv_ref,
    out_ref,
    qs,
    cots,
    kv_all,
    pr_all,
    m_ref,
    l_ref,
    d_ref,
    dq_acc,
    own,
    gsend,
    grecv,
    pacc,
    ps1,
    pr1,
    ps2,
    pr2,
    pg_all,
    weights,
    opart,
    xs,
    xr,
    og,
    w_sem,
    c_send,
    c_recv,
    a_send,
    a_recv,
    b_send,
    b_recv,
    g_send,
    g_recv,
    r1_send,
    r1_recv,
    r2_send,
    r2_recv,
    r3_send,
    r3_recv,
    x_send,
    x_recv,
    o_send,
    o_recv,
):
    n, G, T = sizes
    p = lax.axis_index("prefix")
    g = lax.axis_index("group")
    t = lax.axis_index("tensor")
    L, R, heads, E = q_ref.shape
    pairs = kv_ref.shape[0]
    H = pairs // R
    F = heads // H
    rows = L * F
    piece = pr_ref.shape[3]
    quarter = weights.shape[2]
    scale = 1.0 / math.sqrt(E)
    log_scale = scale * log2_e

    def at(pp=None, gg=None, tt=None):
        return (p if pp is None else pp, g if gg is None else gg, t if tt is None else tt)

    def peer(me, o, size):
        return lax.rem(me + o, size)

    def remote(src, dst, send, recv, where):
        return pltpu.make_async_remote_copy(
            src_ref=src, dst_ref=dst, send_sem=send, recv_sem=recv, device_id=where, device_id_type=MESH
        )

    barrier = pltpu.get_barrier_semaphore()
    for o in range(1, n):
        pl.semaphore_signal(barrier, inc=1, device_id=at(pp=peer(p, o, n)), device_id_type=MESH)
    for o in range(1, G):
        pl.semaphore_signal(barrier, inc=1, device_id=at(gg=peer(g, o, G)), device_id_type=MESH)
    for o in range(1, T):
        pl.semaphore_signal(barrier, inc=1, device_id=at(tt=peer(t, o, T)), device_id_type=MESH)

    half = quarter * G

    def weight_copies():
        copies = []
        for which, ref in enumerate((km_ref, vm_ref)):
            for tt in range(T):
                start = pl.multiple_of(tt * half + g * quarter, 16)
                copies.append(
                    pltpu.make_async_copy(
                        ref.at[pl.ds(start, quarter)], weights.at[which, tt], w_sem.at[which, tt]
                    )
                )
        return copies

    for copy in weight_copies():
        copy.start()

    pl.semaphore_wait(barrier, n + G + T - 3)

    def chunk_copy(src, j):
        return remote(src, kv_all.at[j], c_send.at[j], c_recv.at[j], at(pp=lax.rem(p + 1, n)))

    @pl.when(p < n - 1)
    def _():
        chunk_copy(kv_ref, p).start()

    def prompt_a(o):
        dest = peer(p, o, n)
        return remote(pr_ref.at[g], pr_all.at[p, g], a_send.at[dest], a_recv.at[p], at(pp=dest))

    def prompt_a_wait(o):
        src = peer(p, o, n)
        remote(pr_ref.at[g], pr_all.at[src, g], a_send.at[src], a_recv.at[src], at(pp=src)).wait_recv()

    for o in range(1, n):
        prompt_a(o).start()

    pos = p * L + lax.broadcasted_iota(jnp.int32, (L, F, E), 0)
    for r in range(R):
        length = len_ref[g * R + r]
        q = q_ref[:, r].astype(jnp.float32)
        c = cot_ref[:, r].astype(jnp.float32)
        for h in range(H):
            qs[r * H + h] = q[:, h * F : (h + 1) * F].reshape(rows, E).astype(jnp.bfloat16)
            live = jnp.where(pos < length, c[:, h * F : (h + 1) * F], 0.0)
            cots[r * H + h] = live.reshape(rows, E).astype(jnp.bfloat16)
    pr_all[p] = pr_ref[...]

    def scores(pair, k, diag):
        s = dot_nt(k, qs[pair]) * log_scale
        if diag:
            key = lax.broadcasted_iota(jnp.int32, s.shape, 0)
            query = lax.broadcasted_iota(jnp.int32, s.shape, 1) // F
            s = jnp.where(key <= query, s, masked_score)
        return s

    def stats(pair, k, v, diag):
        s = scores(pair, k, diag)
        dp = dot_nt(v, cots[pair])
        if diag:
            m_new = jnp.max(s, axis=0, keepdims=True)
            e = jnp.exp2(s - m_new)
            l_ref[pair] = jnp.sum(e, axis=0, keepdims=True)
            d_ref[pair] = jnp.sum(e * dp, axis=0, keepdims=True)
        else:
            m_old = m_ref[pair]
            m_new = jnp.maximum(m_old, jnp.max(s, axis=0, keepdims=True))
            e = jnp.exp2(s - m_new)
            a = jnp.exp2(m_old - m_new)
            l_ref[pair] = l_ref[pair] * a + jnp.sum(e, axis=0, keepdims=True)
            d_ref[pair] = d_ref[pair] * a + jnp.sum(e * dp, axis=0, keepdims=True)
        m_ref[pair] = m_new

    def each_pair(body):
        def step(i, carry):
            body(i)
            return carry

        lax.fori_loop(0, pairs, step, 0)

    def prompt_block(which, pair):
        return pr_all[:, :, which, lax.rem(pair, H)].reshape(n * G * piece, E)

    each_pair(lambda i: stats(i, kv_ref[i, 0], kv_ref[i, 1], True))

    def prompt_b(o, oo):
        src, dest = peer(p, o, n), peer(g, oo, G)
        return remote(
            pr_all.at[src, g], pr_all.at[src, g], b_send.at[dest, src], b_recv.at[g, src], at(gg=dest)
        )

    def prompt_b_wait(o, oo):
        src, frm = peer(p, o, n), peer(g, oo, G)
        remote(
            pr_all.at[src, frm], pr_all.at[src, frm], b_send.at[frm, src], b_recv.at[frm, src], at(gg=frm)
        ).wait_recv()

    for o in range(1, n):
        prompt_a_wait(o)
        for oo in range(1, G):
            prompt_b(o, oo).start()

    def prompt_stats():
        for o in range(1, n):
            for oo in range(1, G):
                prompt_b_wait(o, oo)
        each_pair(lambda i: stats(i, prompt_block(0, i), prompt_block(1, i), False))

    def chunk_step(s, carry):
        j = p - s
        chunk_copy(kv_ref, j).wait_recv()

        @pl.when(p < n - 1)
        def _():
            chunk_copy(kv_all.at[j], j).start()

        each_pair(lambda i: stats(i, kv_all[j, i, 0], kv_all[j, i, 1], False))
        return carry

    lax.fori_loop(1, jnp.minimum(p, 1) + 1, chunk_step, 0)
    prompt_stats()
    lax.fori_loop(2, p + 1, chunk_step, 0)

    def finish(i):
        d_ref[i] = d_ref[i] / l_ref[i]
        m_ref[i] = m_ref[i] + jnp.log(l_ref[i]) * log2_e
        dq_acc[i] = jnp.zeros((E, rows), jnp.float32)

    each_pair(finish)

    def grads(pair, k, v, diag):
        prob = jnp.exp2(scores(pair, k, diag) - m_ref[pair])
        dp = dot_nt(v, cots[pair])
        ds = (prob * (dp - d_ref[pair])).astype(jnp.bfloat16)
        dv = dot_nn(prob.astype(jnp.bfloat16), cots[pair])
        dk = dot_nn(ds, qs[pair]) * scale
        dq_acc[pair] += dot_nn(k.T, ds)
        return dk, dv

    def grad_copy(j, i):
        return remote(
            gsend.at[j, i], grecv.at[j, i], g_send.at[j, i], g_recv.at[j, i], at(pp=lax.rem(p + n - 1, n))
        )

    def chunk_grads(j, carry):
        def body(i):
            dk, dv = grads(i, kv_all[j, i, 0], kv_all[j, i, 1], False)

            @pl.when(p == n - 1)
            def _():
                gsend[j, i, 0] = dk.astype(jnp.bfloat16)
                gsend[j, i, 1] = dv.astype(jnp.bfloat16)
                grad_copy(j, i).start()

            @pl.when(p < n - 1)
            def _():
                own[j, i, 0] = dk
                own[j, i, 1] = dv

        each_pair(body)
        return carry

    lax.fori_loop(0, jnp.minimum(p, 1), chunk_grads, 0)

    pacc[...] = jnp.zeros_like(pacc)

    def prompt_grads(i):
        dk, dv = grads(i, prompt_block(0, i), prompt_block(1, i), False)
        h = lax.rem(i, H)
        dk = dk.reshape(n, G, piece, E)
        dv = dv.reshape(n, G, piece, E)
        for gg in range(G):
            pacc[gg, :, 0, h] += dk[:, gg]
            pacc[gg, :, 1, h] += dv[:, gg]

    each_pair(prompt_grads)
    ps1[...] = pacc[...].astype(jnp.bfloat16)

    def r1(o):
        dest = peer(g, o, G)
        return remote(ps1.at[dest], pr1.at[g], r1_send.at[dest], r1_recv.at[g], at(gg=dest))

    def r1_wait(o):
        src = peer(g, o, G)
        remote(ps1.at[src], pr1.at[src], r1_send.at[src], r1_recv.at[src], at(gg=src)).wait_recv()

    for o in range(1, G):
        r1(o).start()

    lax.fori_loop(1, p, chunk_grads, 0)

    def own_grads(i):
        dk, dv = grads(i, kv_ref[i, 0], kv_ref[i, 1], True)

        @pl.when(p == n - 1)
        def _():
            dkv_ref[i, 0] = dk.astype(jnp.bfloat16)
            dkv_ref[i, 1] = dv.astype(jnp.bfloat16)

        @pl.when(p < n - 1)
        def _():
            own[p, i, 0] = dk
            own[p, i, 1] = dv

    each_pair(own_grads)

    for o in range(1, G):
        r1_wait(o)
    pacc[g] = functools.reduce(
        lambda a, b: a + b, [pr1[peer(g, o, G)].astype(jnp.float32) for o in range(1, G)], pacc[g]
    )
    ps2[...] = pacc[g].astype(jnp.bfloat16)

    def r2(o):
        dest = peer(p, o, n)
        return remote(ps2.at[dest], pr2.at[p], r2_send.at[dest], r2_recv.at[p], at(pp=dest))

    def r2_wait(o):
        src = peer(p, o, n)
        remote(ps2.at[src], pr2.at[src], r2_send.at[src], r2_recv.at[src], at(pp=src)).wait_recv()

    for o in range(1, n):
        r2(o).start()

    for r in range(R):
        parts = [dq_acc[r * H + h].T.reshape(L, F, E) for h in range(H)]
        dq_ref[:, r] = (jnp.concatenate(parts, axis=1) * scale).astype(jnp.bfloat16)

    def relay(slot):
        j = slot - (n - 1 - p)

        @pl.when((p < n - 1) & (j >= 0))
        def _():
            def body(i):
                grad_copy(j, i).wait_recv()
                total = own[j, i] + grecv[j, i].astype(jnp.float32)
                low = total.astype(jnp.bfloat16)

                @pl.when(j < p)
                def _():
                    gsend[j, i] = low
                    grad_copy(j, i).start()

                @pl.when(j == p)
                def _():
                    dkv_ref[i] = low

            each_pair(body)

    for slot in range(1, n - 2):
        relay(slot)

    for o in range(1, n):
        r2_wait(o)
    total = pacc[g, p]
    for o in range(1, n):
        total = total + pr2[peer(p, o, n)].astype(jnp.float32)
    pg_all[g] = total.astype(jnp.bfloat16)

    def r3(o):
        dest = peer(g, o, G)
        return remote(pg_all.at[g], pg_all.at[g], r3_send.at[dest], r3_recv.at[g], at(gg=dest))

    def r3_wait(o):
        src = peer(g, o, G)
        remote(pg_all.at[src], pg_all.at[src], r3_send.at[src], r3_recv.at[src], at(gg=src)).wait_recv()

    for o in range(1, G):
        r3(o).start()
    for copy in weight_copies():
        copy.wait()
    for o in range(1, G):
        r3_wait(o)

    def project(tt):
        result = None
        for which in range(2):
            for h in range(H):
                low = pg_all[:, which, h].reshape(G * piece, E)
                term = dot_nt(low, weights[which, tt, :, h * E : (h + 1) * E])
                result = term if result is None else result + term
        return result

    def x_copy(o):
        dest = peer(t, o, T)
        return remote(xs.at[o - 1], xr.at[o - 1], x_send.at[o - 1], x_recv.at[o - 1], at(tt=dest))

    for o in range(1, T):
        xs[o - 1] = project(peer(t, o, T)).astype(jnp.bfloat16)
        x_copy(o).start()
    opart[...] = project(t)

    if n > 2:
        relay(n - 2)

    result = opart[...]
    for o in range(1, T):
        x_copy(o).wait_recv()
        result = result + xr[o - 1].astype(jnp.float32)
    og[g] = result.astype(jnp.bfloat16)

    def o_copy(o):
        dest = peer(g, o, G)
        return remote(og.at[g], og.at[g], o_send.at[dest], o_recv.at[g], at(gg=dest))

    def o_wait(o):
        src = peer(g, o, G)
        remote(og.at[src], og.at[src], o_send.at[src], o_recv.at[src], at(gg=src)).wait_recv()

    for o in range(1, G):
        o_copy(o).start()
    relay(n - 1)
    for o in range(1, G):
        o_wait(o)
    for gg in range(G):
        out_ref[:, gg * quarter : (gg + 1) * quarter] = og[gg]

    def chunk_sent(j, carry):
        chunk_copy(kv_ref, j).wait_send()
        return carry

    @pl.when(p < n - 1)
    def _():
        lax.fori_loop(0, p + 1, chunk_sent, 0)

    def grads_sent(j, carry):
        each_pair(lambda i: grad_copy(j, i).wait_send())
        return carry

    lax.fori_loop(0, p, grads_sent, 0)
    for o in range(1, n):
        prompt_a(o).wait_send()
        r2(o).wait_send()
        for oo in range(1, G):
            prompt_b(o, oo).wait_send()
    for o in range(1, G):
        r1(o).wait_send()
        r3(o).wait_send()
        o_copy(o).wait_send()
    for o in range(1, T):
        x_copy(o).wait_send()


def per_device(
    sizes,
    resp_query,
    response_key,
    response_value,
    resp_cotangent,
    prompt_key,
    prompt_value_rows,
    key_matrix,
    value_matrix,
    resp_lengths,
):
    n, G, T = sizes
    L, R, heads, E = resp_query.shape
    H = response_key.shape[2]
    pairs = R * H
    rows = L * heads // H
    prompt_rows = prompt_key.shape[0]
    piece = prompt_rows // G
    width = key_matrix.shape[0]
    quarter = width // T // G
    bf16, f32 = jnp.bfloat16, jnp.float32

    kv = jnp.stack((response_key, response_value), axis=0)
    kv = kv.transpose(2, 3, 0, 1, 4).reshape(pairs, 2, L, E)
    prompt = jnp.stack((prompt_key, prompt_value_rows), axis=0)
    prompt = prompt.reshape(2, G, piece, H, E).transpose(1, 0, 3, 2, 4)

    vmem = pl.BlockSpec(memory_space=pltpu.VMEM)
    dma = pltpu.SemaphoreType.DMA
    scratch = [
        pltpu.VMEM((pairs, rows, E), bf16),
        pltpu.VMEM((pairs, rows, E), bf16),
        pltpu.VMEM((n, pairs, 2, L, E), bf16),
        pltpu.VMEM((n, G, 2, H, piece, E), bf16),
        pltpu.VMEM((pairs, 1, rows), f32),
        pltpu.VMEM((pairs, 1, rows), f32),
        pltpu.VMEM((pairs, 1, rows), f32),
        pltpu.VMEM((pairs, E, rows), f32),
        pltpu.VMEM((n, pairs, 2, L, E), f32),
        pltpu.VMEM((n, pairs, 2, L, E), bf16),
        pltpu.VMEM((n, pairs, 2, L, E), bf16),
        pltpu.VMEM((G, n, 2, H, piece, E), f32),
        pltpu.VMEM((G, n, 2, H, piece, E), bf16),
        pltpu.VMEM((G, n, 2, H, piece, E), bf16),
        pltpu.VMEM((n, 2, H, piece, E), bf16),
        pltpu.VMEM((n, 2, H, piece, E), bf16),
        pltpu.VMEM((G, 2, H, piece, E), bf16),
        pltpu.VMEM((2, T, quarter, H * E), bf16),
        pltpu.VMEM((prompt_rows, quarter), f32),
        pltpu.VMEM((max(T - 1, 1), prompt_rows, quarter), bf16),
        pltpu.VMEM((max(T - 1, 1), prompt_rows, quarter), bf16),
        pltpu.VMEM((G, prompt_rows, quarter), bf16),
        dma((2, T)),
        dma((n,)),
        dma((n,)),
        dma((n,)),
        dma((n,)),
        dma((G, n)),
        dma((G, n)),
        dma((n, pairs)),
        dma((n, pairs)),
        dma((G,)),
        dma((G,)),
        dma((n,)),
        dma((n,)),
        dma((G,)),
        dma((G,)),
        dma((max(T - 1, 1),)),
        dma((max(T - 1, 1),)),
        dma((G,)),
        dma((G,)),
    ]
    query_grad, kv_grad, out = pl.pallas_call(
        functools.partial(kernel, sizes),
        out_shape=(
            jax.ShapeDtypeStruct((L, R, heads, E), bf16),
            jax.ShapeDtypeStruct((pairs, 2, L, E), bf16),
            jax.ShapeDtypeStruct((prompt_rows, width // T), bf16),
        ),
        in_specs=[
            pl.BlockSpec(memory_space=pltpu.SMEM),
            vmem,
            vmem,
            vmem,
            vmem,
            pl.BlockSpec(memory_space=pl.ANY),
            pl.BlockSpec(memory_space=pl.ANY),
        ],
        out_specs=(vmem, vmem, vmem),
        scratch_shapes=scratch,
        compiler_params=pltpu.CompilerParams(
            collective_id=0, has_side_effects=True, vmem_limit_bytes=60 * 1024 * 1024
        ),
    )(resp_lengths, kv, prompt, resp_query, resp_cotangent, key_matrix, value_matrix)
    kv_grad = kv_grad.reshape(R, H, 2, L, E).transpose(2, 3, 0, 1, 4)
    return (query_grad, kv_grad[0], kv_grad[1], out)


def solution(mesh):
    sizes = (mesh.shape["prefix"], mesh.shape["group"], mesh.shape["tensor"])
    placed = (
        P("prefix", "group", "tensor", None),
        P("prefix", "group", "tensor", None),
        P("prefix", "group", "tensor", None),
        P("prefix", "group", "tensor", None),
        P("prefix", "tensor", None),
        P("prefix", "tensor", None),
        P(None, "tensor"),
        P(None, "tensor"),
        P(),
    )
    return jax.shard_map(
        functools.partial(per_device, sizes),
        mesh=mesh,
        in_specs=placed,
        out_specs=(
            P("prefix", "group", "tensor", None),
            P("prefix", "group", "tensor", None),
            P("prefix", "group", "tensor", None),
            P("prefix", "tensor"),
        ),
        check_vma=False,
    )
```

```python
import functools
import math

import jax
import jax.numpy as jnp
from jax import lax
from jax.experimental import pallas as pl
from jax.experimental.pallas import tpu as pltpu
from jax.sharding import PartitionSpec as P

MESH = pl.DeviceIdType.MESH
masked_score = -1e30
log2_e = math.log2(math.e)


def dot_nt(a, b):
    return lax.dot_general(a, b, (((1,), (1,)), ((), ())), preferred_element_type=jnp.float32)


def dot_nn(a, b):
    return lax.dot_general(a, b, (((1,), (0,)), ((), ())), preferred_element_type=jnp.float32)


def kernel(
    sizes,
    len_ref,
    key_ref,
    value_ref,
    pkey_ref,
    pvalue_ref,
    q_hbm,
    cot_hbm,
    km_ref,
    vm_ref,
    dq_hbm,
    dkey_ref,
    dvalue_ref,
    out_ref,
    q_ref,
    cot_ref,
    dq_ref,
    wide,
    kv_ref,
    pr_ref,
    qs,
    cots,
    qts,
    cotts,
    kv_all,
    pr_all,
    m_ref,
    l_ref,
    d_ref,
    dq_acc,
    own,
    gsend,
    grecv,
    pacc,
    ps1,
    pr1,
    ps2,
    pr2,
    pg_all,
    weights,
    opart,
    xs,
    xr,
    og,
    w_sem,
    q_sem,
    c_send,
    c_recv,
    a_send,
    a_recv,
    b_send,
    b_recv,
    g_send,
    g_recv,
    r1_send,
    r1_recv,
    r2_send,
    r2_recv,
    r3_send,
    r3_recv,
    x_send,
    x_recv,
    o_send,
    o_recv,
):
    n, G, T = sizes
    p = lax.axis_index("prefix")
    g = lax.axis_index("group")
    t = lax.axis_index("tensor")
    L, R, heads, E = q_ref.shape
    pairs = kv_ref.shape[0]
    H = pairs // R
    F = heads // H
    rows = L * F
    piece = pr_ref.shape[3]
    quarter = weights.shape[2]
    scale = 1.0 / math.sqrt(E)
    log_scale = scale * log2_e

    def at(pp=None, gg=None, tt=None):
        return (p if pp is None else pp, g if gg is None else gg, t if tt is None else tt)

    def peer(me, o, size):
        return lax.rem(me + o, size)

    def remote(src, dst, send, recv, where):
        return pltpu.make_async_remote_copy(
            src_ref=src, dst_ref=dst, send_sem=send, recv_sem=recv, device_id=where, device_id_type=MESH
        )

    barrier = pltpu.get_barrier_semaphore()
    for o in range(1, n):
        pl.semaphore_signal(barrier, inc=1, device_id=at(pp=peer(p, o, n)), device_id_type=MESH)
    for o in range(1, G):
        pl.semaphore_signal(barrier, inc=1, device_id=at(gg=peer(g, o, G)), device_id_type=MESH)
    for o in range(1, T):
        pl.semaphore_signal(barrier, inc=1, device_id=at(tt=peer(t, o, T)), device_id_type=MESH)

    half = quarter * G

    def weight_copies():
        copies = []
        for which, ref in enumerate((km_ref, vm_ref)):
            for tt in range(T):
                start = pl.multiple_of(tt * half + g * quarter, 16)
                copies.append(
                    pltpu.make_async_copy(
                        ref.at[pl.ds(start, quarter)], weights.at[which, tt], w_sem.at[which, tt]
                    )
                )
        return copies

    in_copies = (
        pltpu.make_async_copy(q_hbm, q_ref, q_sem.at[0]),
        pltpu.make_async_copy(cot_hbm, cot_ref, q_sem.at[1]),
    )
    out_copy = pltpu.make_async_copy(dq_ref, dq_hbm, q_sem.at[2])
    for copy in in_copies:
        copy.start()
    for copy in weight_copies():
        copy.start()

    for which, ref in enumerate((key_ref, value_ref)):
        wide[which] = ref[...].astype(jnp.float32)
        for i in range(pairs):
            kv_ref[i, which] = wide[which, pl.ds(i, L, stride=pairs), :].astype(jnp.bfloat16)
    for which, ref in enumerate((pkey_ref, pvalue_ref)):
        wide[which, : G * piece * H] = ref[...].astype(jnp.float32)
        for gg in range(G):
            for h in range(H):
                rows_of = pl.ds(gg * piece * H + h, piece, stride=H)
                pr_ref[gg, which, h] = wide[which, rows_of, :].astype(jnp.bfloat16)

    pl.semaphore_wait(barrier, n + G + T - 3)

    def chunk_copy(src, j):
        return remote(src, kv_all.at[j], c_send.at[j], c_recv.at[j], at(pp=lax.rem(p + 1, n)))

    @pl.when(p < n - 1)
    def _():
        chunk_copy(kv_ref, p).start()

    def prompt_a(o):
        dest = peer(p, o, n)
        return remote(pr_ref.at[g], pr_all.at[p, g], a_send.at[dest], a_recv.at[p], at(pp=dest))

    def prompt_a_wait(o):
        src = peer(p, o, n)
        remote(pr_ref.at[g], pr_all.at[src, g], a_send.at[src], a_recv.at[src], at(pp=src)).wait_recv()

    for o in range(1, n):
        prompt_a(o).start()

    pos = p * L + lax.broadcasted_iota(jnp.int32, (L, F, E), 0)
    for copy in in_copies:
        copy.wait()
    for r in range(R):
        length = len_ref[g * R + r]
        q = q_ref[:, r].astype(jnp.float32)
        c = cot_ref[:, r].astype(jnp.float32)
        for h in range(H):
            part = q[:, h * F : (h + 1) * F].reshape(rows, E)
            qs[r * H + h] = part.astype(jnp.bfloat16)
            qts[r * H + h] = part.T.astype(jnp.bfloat16)
            live = jnp.where(pos < length, c[:, h * F : (h + 1) * F], 0.0).reshape(rows, E)
            cots[r * H + h] = live.astype(jnp.bfloat16)
            cotts[r * H + h] = live.T.astype(jnp.bfloat16)
    pr_all[p] = pr_ref[...]

    def scores(pair, k, diag):
        s = dot_nn(k, qts[pair]) * log_scale
        if diag:
            key = lax.broadcasted_iota(jnp.int32, s.shape, 0)
            query = lax.broadcasted_iota(jnp.int32, s.shape, 1) // F
            s = jnp.where(key <= query, s, masked_score)
        return s

    def stats(pair, k, v, diag):
        s = scores(pair, k, diag)
        dp = dot_nn(v, cotts[pair])
        if diag:
            m_new = jnp.max(s, axis=0, keepdims=True)
            e = jnp.exp2(s - m_new)
            l_ref[pair] = jnp.sum(e, axis=0, keepdims=True)
            d_ref[pair] = jnp.sum(e * dp, axis=0, keepdims=True)
        else:
            m_old = m_ref[pair]
            m_new = jnp.maximum(m_old, jnp.max(s, axis=0, keepdims=True))
            e = jnp.exp2(s - m_new)
            a = jnp.exp2(m_old - m_new)
            l_ref[pair] = l_ref[pair] * a + jnp.sum(e, axis=0, keepdims=True)
            d_ref[pair] = d_ref[pair] * a + jnp.sum(e * dp, axis=0, keepdims=True)
        m_ref[pair] = m_new

    together = 2 if pairs % 2 == 0 else 1

    def each_pair(body, after=None):
        def step(i, carry):
            for k in range(together):
                body(i * together + k)
            if after is not None:
                for k in range(together):
                    after(i * together + k)
            return carry

        lax.fori_loop(0, pairs // together, step, 0)

    def prompt_block(which, pair):
        return pr_all[:, :, which, lax.rem(pair, H)].reshape(n * G * piece, E)

    each_pair(lambda i: stats(i, kv_ref[i, 0], kv_ref[i, 1], True))

    def prompt_b(o, oo):
        src, dest = peer(p, o, n), peer(g, oo, G)
        return remote(
            pr_all.at[src, g], pr_all.at[src, g], b_send.at[dest, src], b_recv.at[g, src], at(gg=dest)
        )

    def prompt_b_wait(o, oo):
        src, frm = peer(p, o, n), peer(g, oo, G)
        remote(
            pr_all.at[src, frm], pr_all.at[src, frm], b_send.at[frm, src], b_recv.at[frm, src], at(gg=frm)
        ).wait_recv()

    for o in range(1, n):
        prompt_a_wait(o)
        for oo in range(1, G):
            prompt_b(o, oo).start()

    def prompt_stats():
        for o in range(1, n):
            for oo in range(1, G):
                prompt_b_wait(o, oo)
        each_pair(lambda i: stats(i, prompt_block(0, i), prompt_block(1, i), False))

    def chunk_step(s, carry):
        j = p - s
        chunk_copy(kv_ref, j).wait_recv()

        @pl.when(p < n - 1)
        def _():
            chunk_copy(kv_all.at[j], j).start()

        each_pair(lambda i: stats(i, kv_all[j, i, 0], kv_all[j, i, 1], False))
        return carry

    lax.fori_loop(1, jnp.minimum(p, 1) + 1, chunk_step, 0)
    prompt_stats()
    lax.fori_loop(2, p + 1, chunk_step, 0)

    def finish(i):
        d_ref[i] = d_ref[i] / l_ref[i]
        m_ref[i] = m_ref[i] + jnp.log(l_ref[i]) * log2_e
        dq_acc[i] = jnp.zeros((E, rows), jnp.float32)

    each_pair(finish)

    def grads(pair, k, v, diag):
        prob = jnp.exp2(scores(pair, k, diag) - m_ref[pair])
        dp = dot_nn(v, cotts[pair])
        ds = (prob * (dp - d_ref[pair])).astype(jnp.bfloat16)
        dv = dot_nn(prob.astype(jnp.bfloat16), cots[pair])
        dk = dot_nn(ds, qs[pair]) * scale
        dq_acc[pair] += dot_nn(k.T, ds)
        return dk, dv

    def grad_copy(j, i):
        return remote(
            gsend.at[j, i], grecv.at[j, i], g_send.at[j, i], g_recv.at[j, i], at(pp=lax.rem(p + n - 1, n))
        )

    def chunk_grads(j, carry):
        def body(i):
            dk, dv = grads(i, kv_all[j, i, 0], kv_all[j, i, 1], False)
            gsend[j, i, 0] = dk.astype(jnp.bfloat16)
            gsend[j, i, 1] = dv.astype(jnp.bfloat16)
            own[j, i, 0] = dk
            own[j, i, 1] = dv

        def after(i):
            @pl.when(p == n - 1)
            def _():
                grad_copy(j, i).start()

        each_pair(body, after)
        return carry

    lax.fori_loop(0, jnp.minimum(p, 1), chunk_grads, 0)

    pacc[...] = jnp.zeros_like(pacc)

    def prompt_grads(i):
        dk, dv = grads(i, prompt_block(0, i), prompt_block(1, i), False)
        h = lax.rem(i, H)
        dk = dk.reshape(n, G, piece, E)
        dv = dv.reshape(n, G, piece, E)
        for gg in range(G):
            pacc[gg, :, 0, h] += dk[:, gg]
            pacc[gg, :, 1, h] += dv[:, gg]

    each_pair(prompt_grads)
    ps1[...] = pacc[...].astype(jnp.bfloat16)

    def r1(o):
        dest = peer(g, o, G)
        return remote(ps1.at[dest], pr1.at[g], r1_send.at[dest], r1_recv.at[g], at(gg=dest))

    def r1_wait(o):
        src = peer(g, o, G)
        remote(ps1.at[src], pr1.at[src], r1_send.at[src], r1_recv.at[src], at(gg=src)).wait_recv()

    for o in range(1, G):
        r1(o).start()

    lax.fori_loop(1, p - 1, chunk_grads, 0)

    for o in range(1, G):
        r1_wait(o)
    pacc[g] = functools.reduce(
        lambda a, b: a + b, [pr1[peer(g, o, G)].astype(jnp.float32) for o in range(1, G)], pacc[g]
    )
    ps2[...] = pacc[g].astype(jnp.bfloat16)

    def r2(o):
        dest = peer(p, o, n)
        return remote(ps2.at[dest], pr2.at[p], r2_send.at[dest], r2_recv.at[p], at(pp=dest))

    def r2_wait(o):
        src = peer(p, o, n)
        remote(ps2.at[src], pr2.at[src], r2_send.at[src], r2_recv.at[src], at(pp=src)).wait_recv()

    for o in range(1, n):
        r2(o).start()

    lax.fori_loop(jnp.maximum(p - 1, 1), p, chunk_grads, 0)

    def relay(slot):
        j = slot - (n - 1 - p)

        @pl.when((p < n - 1) & (j >= 0))
        def _():
            def body(i):
                grad_copy(j, i).wait_recv()
                total = own[j, i] + grecv[j, i].astype(jnp.float32)

                @pl.when(j < p)
                def _():
                    gsend[j, i] = total.astype(jnp.bfloat16)
                    grad_copy(j, i).start()

                @pl.when(j == p)
                def _():
                    own[j, i] = total

            each_pair(body)

    for slot in range(1, n - 2):
        relay(slot)

    for o in range(1, n):
        r2_wait(o)
    total = pacc[g, p]
    for o in range(1, n):
        total = total + pr2[peer(p, o, n)].astype(jnp.float32)
    pg_all[g] = total.astype(jnp.bfloat16)

    def r3(o):
        dest = peer(g, o, G)
        return remote(pg_all.at[g], pg_all.at[g], r3_send.at[dest], r3_recv.at[g], at(gg=dest))

    def r3_wait(o):
        src = peer(g, o, G)
        remote(pg_all.at[src], pg_all.at[src], r3_send.at[src], r3_recv.at[src], at(gg=src)).wait_recv()

    for o in range(1, G):
        r3(o).start()

    def own_grads(i):
        dk, dv = grads(i, kv_ref[i, 0], kv_ref[i, 1], True)
        own[p, i, 0] = dk
        own[p, i, 1] = dv

    each_pair(own_grads)

    for copy in weight_copies():
        copy.wait()
    for o in range(1, G):
        r3_wait(o)

    def project(tt):
        result = None
        for which in range(2):
            for h in range(H):
                low = pg_all[:, which, h].reshape(G * piece, E)
                term = dot_nt(low, weights[which, tt, :, h * E : (h + 1) * E])
                result = term if result is None else result + term
        return result

    def x_copy(o):
        dest = peer(t, o, T)
        return remote(xs.at[o - 1], xr.at[o - 1], x_send.at[o - 1], x_recv.at[o - 1], at(tt=dest))

    for o in range(1, T):
        xs[o - 1] = project(peer(t, o, T)).astype(jnp.bfloat16)
        x_copy(o).start()
    opart[...] = project(t)

    for r in range(R):
        parts = [dq_acc[r * H + h].T.reshape(L, F, E) for h in range(H)]
        dq_ref[:, r] = (jnp.concatenate(parts, axis=1) * scale).astype(jnp.bfloat16)
    out_copy.start()

    if n > 2:
        relay(n - 2)

    result = opart[...]
    for o in range(1, T):
        x_copy(o).wait_recv()
        result = result + xr[o - 1].astype(jnp.float32)
    og[g] = result.astype(jnp.bfloat16)

    def o_copy(o):
        dest = peer(g, o, G)
        return remote(og.at[g], og.at[g], o_send.at[dest], o_recv.at[g], at(gg=dest))

    def o_wait(o):
        src = peer(g, o, G)
        remote(og.at[src], og.at[src], o_send.at[src], o_recv.at[src], at(gg=src)).wait_recv()

    for o in range(1, G):
        o_copy(o).start()
    relay(n - 1)
    for which, ref in enumerate((dkey_ref, dvalue_ref)):
        for i in range(pairs):
            wide[which, pl.ds(i, L, stride=pairs), :] = own[p, i, which]
        ref[...] = wide[which].astype(jnp.bfloat16)
    for o in range(1, G):
        o_wait(o)
    for gg in range(G):
        out_ref[:, gg * quarter : (gg + 1) * quarter] = og[gg]
    out_copy.wait()

    def chunk_sent(j, carry):
        chunk_copy(kv_ref, j).wait_send()
        return carry

    @pl.when(p < n - 1)
    def _():
        lax.fori_loop(0, p + 1, chunk_sent, 0)

    def grads_sent(j, carry):
        each_pair(lambda i: grad_copy(j, i).wait_send())
        return carry

    lax.fori_loop(0, p, grads_sent, 0)
    for o in range(1, n):
        prompt_a(o).wait_send()
        r2(o).wait_send()
        for oo in range(1, G):
            prompt_b(o, oo).wait_send()
    for o in range(1, G):
        r1(o).wait_send()
        r3(o).wait_send()
        o_copy(o).wait_send()
    for o in range(1, T):
        x_copy(o).wait_send()


def hand_on(*refs):
    sem = refs[8]
    copies = [pltpu.make_async_copy(refs[i], refs[4 + i], sem.at[i]) for i in range(4)]
    for copy in copies:
        copy.start()
    for copy in copies:
        copy.wait()


def per_device(
    sizes,
    resp_query,
    response_key,
    response_value,
    resp_cotangent,
    prompt_key,
    prompt_value_rows,
    key_matrix,
    value_matrix,
    resp_lengths,
):
    n, G, T = sizes
    L, R, heads, E = resp_query.shape
    H = response_key.shape[2]
    pairs = R * H
    rows = L * heads // H
    prompt_rows = prompt_key.shape[0]
    piece = prompt_rows // G
    width = key_matrix.shape[0]
    quarter = width // T // G
    bf16, f32 = jnp.bfloat16, jnp.float32

    vmem = pl.BlockSpec(memory_space=pltpu.VMEM)
    anywhere = pl.BlockSpec(memory_space=pl.ANY)
    dma = pltpu.SemaphoreType.DMA
    scratch = [
        pltpu.VMEM((L, R, heads, E), bf16),
        pltpu.VMEM((L, R, heads, E), bf16),
        pltpu.VMEM((L, R, heads, E), bf16),
        pltpu.VMEM((2, max(L * pairs, prompt_rows * H), E), f32),
        pltpu.VMEM((pairs, 2, L, E), bf16),
        pltpu.VMEM((G, 2, H, piece, E), bf16),
        pltpu.VMEM((pairs, rows, E), bf16),
        pltpu.VMEM((pairs, rows, E), bf16),
        pltpu.VMEM((pairs, E, rows), bf16),
        pltpu.VMEM((pairs, E, rows), bf16),
        pltpu.VMEM((n, pairs, 2, L, E), bf16),
        pltpu.VMEM((n, G, 2, H, piece, E), bf16),
        pltpu.VMEM((pairs, 1, rows), f32),
        pltpu.VMEM((pairs, 1, rows), f32),
        pltpu.VMEM((pairs, 1, rows), f32),
        pltpu.VMEM((pairs, E, rows), f32),
        pltpu.VMEM((n, pairs, 2, L, E), f32),
        pltpu.VMEM((n, pairs, 2, L, E), bf16),
        pltpu.VMEM((n, pairs, 2, L, E), bf16),
        pltpu.VMEM((G, n, 2, H, piece, E), f32),
        pltpu.VMEM((G, n, 2, H, piece, E), bf16),
        pltpu.VMEM((G, n, 2, H, piece, E), bf16),
        pltpu.VMEM((n, 2, H, piece, E), bf16),
        pltpu.VMEM((n, 2, H, piece, E), bf16),
        pltpu.VMEM((G, 2, H, piece, E), bf16),
        pltpu.VMEM((2, T, quarter, H * E), bf16),
        pltpu.VMEM((prompt_rows, quarter), f32),
        pltpu.VMEM((max(T - 1, 1), prompt_rows, quarter), bf16),
        pltpu.VMEM((max(T - 1, 1), prompt_rows, quarter), bf16),
        pltpu.VMEM((G, prompt_rows, quarter), bf16),
        dma((2, T)),
        dma((3,)),
        dma((n,)),
        dma((n,)),
        dma((n,)),
        dma((n,)),
        dma((G, n)),
        dma((G, n)),
        dma((n, pairs)),
        dma((n, pairs)),
        dma((G,)),
        dma((G,)),
        dma((n,)),
        dma((n,)),
        dma((G,)),
        dma((G,)),
        dma((max(T - 1, 1),)),
        dma((max(T - 1, 1),)),
        dma((G,)),
        dma((G,)),
    ]
    results = pl.pallas_call(
        functools.partial(kernel, sizes),
        out_shape=(
            jax.ShapeDtypeStruct((L, R, heads, E), bf16),
            jax.ShapeDtypeStruct((L * pairs, E), bf16),
            jax.ShapeDtypeStruct((L * pairs, E), bf16),
            jax.ShapeDtypeStruct((prompt_rows, width // T), bf16),
        ),
        in_specs=[pl.BlockSpec(memory_space=pltpu.SMEM)] + [vmem] * 4 + [anywhere] * 4,
        out_specs=(anywhere, vmem, vmem, vmem),
        scratch_shapes=scratch,
        compiler_params=pltpu.CompilerParams(
            collective_id=0, has_side_effects=True, vmem_limit_bytes=60 * 1024 * 1024
        ),
    )(
        resp_lengths,
        response_key.reshape(L * pairs, E),
        response_value.reshape(L * pairs, E),
        prompt_key.reshape(prompt_rows * H, E),
        prompt_value_rows.reshape(prompt_rows * H, E),
        resp_query,
        resp_cotangent,
        key_matrix,
        value_matrix,
    )
    query_grad, key_grad, value_grad, out = pl.pallas_call(
        hand_on,
        out_shape=tuple(jax.ShapeDtypeStruct(x.shape, x.dtype) for x in results),
        in_specs=[anywhere] * 4,
        out_specs=(anywhere,) * 4,
        scratch_shapes=[dma((4,))],
        compiler_params=pltpu.CompilerParams(vmem_limit_bytes=60 * 1024 * 1024),
    )(*results)
    shape = response_key.shape
    return (query_grad, key_grad.reshape(shape), value_grad.reshape(shape), out)


def solution(mesh):
    sizes = (mesh.shape["prefix"], mesh.shape["group"], mesh.shape["tensor"])
    placed = (
        P("prefix", "group", "tensor", None),
        P("prefix", "group", "tensor", None),
        P("prefix", "group", "tensor", None),
        P("prefix", "group", "tensor", None),
        P("prefix", "tensor", None),
        P("prefix", "tensor", None),
        P(None, "tensor"),
        P(None, "tensor"),
        P(),
    )
    return jax.shard_map(
        functools.partial(per_device, sizes),
        mesh=mesh,
        in_specs=placed,
        out_specs=(
            P("prefix", "group", "tensor", None),
            P("prefix", "group", "tensor", None),
            P("prefix", "group", "tensor", None),
            P("prefix", "tensor"),
        ),
        check_vma=False,
    )
```

```python
import functools
import math

import jax
import jax.numpy as jnp
from jax import lax
from jax.experimental import pallas as pl
from jax.experimental.pallas import tpu as pltpu
from jax.sharding import PartitionSpec as P

MESH = pl.DeviceIdType.MESH
masked_score = -1e30
log2_e = math.log2(math.e)


def dot_nt(a, b):
    return lax.dot_general(a, b, (((1,), (1,)), ((), ())), preferred_element_type=jnp.float32)


def dot_nn(a, b):
    return lax.dot_general(a, b, (((1,), (0,)), ((), ())), preferred_element_type=jnp.float32)


def kernel(
    sizes,
    len_ref,
    key_ref,
    value_ref,
    pkey_ref,
    pvalue_ref,
    q_hbm,
    cot_hbm,
    km_ref,
    vm_ref,
    dq_hbm,
    dkey_ref,
    dvalue_ref,
    out_ref,
    q_ref,
    cot_ref,
    dq_ref,
    wide,
    kv_ref,
    pr_ref,
    qs,
    cots,
    qts,
    cotts,
    kv_all,
    pr_all,
    s_buf,
    dp_buf,
    m_ref,
    l_ref,
    d_ref,
    dq_acc,
    own,
    gsend,
    grecv,
    pacc,
    ps1,
    pr1,
    ps2,
    pr2,
    pg_all,
    weights,
    opart,
    xs,
    xr,
    og,
    w_sem,
    q_sem,
    c_send,
    c_recv,
    a_send,
    a_recv,
    b_send,
    b_recv,
    g_send,
    g_recv,
    r1_send,
    r1_recv,
    r2_send,
    r2_recv,
    r3_send,
    r3_recv,
    x_send,
    x_recv,
    o_send,
    o_recv,
):
    n, G, T = sizes
    p = lax.axis_index("prefix")
    g = lax.axis_index("group")
    t = lax.axis_index("tensor")
    L, R, heads, E = q_ref.shape
    pairs = kv_ref.shape[0]
    H = pairs // R
    F = heads // H
    rows = L * F
    piece = pr_ref.shape[3]
    quarter = weights.shape[2]
    scale = 1.0 / math.sqrt(E)
    log_scale = scale * log2_e

    def at(pp=None, gg=None, tt=None):
        return (p if pp is None else pp, g if gg is None else gg, t if tt is None else tt)

    def peer(me, o, size):
        return lax.rem(me + o, size)

    def remote(src, dst, send, recv, where):
        return pltpu.make_async_remote_copy(
            src_ref=src, dst_ref=dst, send_sem=send, recv_sem=recv, device_id=where, device_id_type=MESH
        )

    barrier = pltpu.get_barrier_semaphore()
    for o in range(1, n):
        pl.semaphore_signal(barrier, inc=1, device_id=at(pp=peer(p, o, n)), device_id_type=MESH)
    for o in range(1, G):
        pl.semaphore_signal(barrier, inc=1, device_id=at(gg=peer(g, o, G)), device_id_type=MESH)
    for o in range(1, T):
        pl.semaphore_signal(barrier, inc=1, device_id=at(tt=peer(t, o, T)), device_id_type=MESH)

    half = quarter * G

    def weight_copies():
        copies = []
        for which, ref in enumerate((km_ref, vm_ref)):
            for tt in range(T):
                start = pl.multiple_of(tt * half + g * quarter, 16)
                copies.append(
                    pltpu.make_async_copy(
                        ref.at[pl.ds(start, quarter)], weights.at[which, tt], w_sem.at[which, tt]
                    )
                )
        return copies

    in_copies = (
        pltpu.make_async_copy(q_hbm, q_ref, q_sem.at[0]),
        pltpu.make_async_copy(cot_hbm, cot_ref, q_sem.at[1]),
    )
    out_copy = pltpu.make_async_copy(dq_ref, dq_hbm, q_sem.at[2])
    for copy in in_copies:
        copy.start()
    for copy in weight_copies():
        copy.start()

    for which, ref in enumerate((key_ref, value_ref)):
        wide[which, : L * pairs] = ref[...].astype(jnp.float32)
        for i in range(pairs):
            kv_ref[i, which] = wide[which, pl.ds(i, L, stride=pairs), :].astype(jnp.bfloat16)
    for which, ref in enumerate((pkey_ref, pvalue_ref)):
        wide[which, : G * piece * H] = ref[...].astype(jnp.float32)
        for gg in range(G):
            for h in range(H):
                rows_of = pl.ds(gg * piece * H + h, piece, stride=H)
                pr_ref[gg, which, h] = wide[which, rows_of, :].astype(jnp.bfloat16)

    pl.semaphore_wait(barrier, n + G + T - 3)

    def order(k):
        return lax.rem(k, R) * H + k // R

    def chunk_copy(dest, i):
        return remote(kv_ref.at[i], kv_all.at[p, i], c_send.at[dest, i], c_recv.at[p, i], at(pp=dest))

    def chunk_wait(j, i):
        remote(kv_ref.at[i], kv_all.at[j, i], c_send.at[j, i], c_recv.at[j, i], at(pp=j)).wait_recv()

    def prompt_a(o):
        dest = peer(p, o, n)
        return remote(pr_ref.at[g], pr_all.at[p, g], a_send.at[dest], a_recv.at[p], at(pp=dest))

    def prompt_a_wait(o):
        src = peer(p, o, n)
        remote(pr_ref.at[g], pr_all.at[src, g], a_send.at[src], a_recv.at[src], at(pp=src)).wait_recv()

    for o in range(1, n):
        prompt_a(o).start()

    def send_pair(k, carry):
        def send_to(d, inner):
            chunk_copy(n - 1 - d, order(k)).start()
            return inner

        return lax.fori_loop(0, n - 1 - p, send_to, carry)

    lax.fori_loop(0, pairs, send_pair, 0)

    def prompt_b(o, oo):
        src, dest = peer(p, o, n), peer(g, oo, G)
        return remote(
            pr_all.at[src, g], pr_all.at[src, g], b_send.at[dest, src], b_recv.at[g, src], at(gg=dest)
        )

    def prompt_b_wait(o, oo):
        src, frm = peer(p, o, n), peer(g, oo, G)
        remote(
            pr_all.at[src, frm], pr_all.at[src, frm], b_send.at[frm, src], b_recv.at[frm, src], at(gg=frm)
        ).wait_recv()

    pr_all[p] = pr_ref[...]
    pos = p * L + lax.broadcasted_iota(jnp.int32, (L, F, E), 0)
    for copy in in_copies:
        copy.wait()
    for r in range(R):
        length = len_ref[g * R + r]
        q = q_ref[:, r].astype(jnp.float32)
        c = cot_ref[:, r].astype(jnp.float32)
        for h in range(H):
            part = q[:, h * F : (h + 1) * F].reshape(rows, E)
            qs[r * H + h] = part.astype(jnp.bfloat16)
            qts[r * H + h] = part.T.astype(jnp.bfloat16)
            live = jnp.where(pos < length, c[:, h * F : (h + 1) * F], 0.0).reshape(rows, E)
            cots[r * H + h] = live.astype(jnp.bfloat16)
            cotts[r * H + h] = live.T.astype(jnp.bfloat16)
        if r == 0:
            for o in range(1, n):
                prompt_a_wait(o)
                for oo in range(1, G):
                    prompt_b(o, oo).start()
    for o in range(1, n):
        for oo in range(1, G):
            prompt_b_wait(o, oo)

    prompt_keys = n * G * piece

    def prompt_block(which, pair):
        return pr_all[:, :, which, lax.rem(pair, H)].reshape(prompt_keys, E)

    def block(j):
        return pl.ds(pl.multiple_of(j * L, L), L)

    prompt_rows = pl.ds(n * L, prompt_keys)

    def stats(pair, where, k, v, diag):
        s = dot_nn(k, qts[pair]) * log_scale
        if diag:
            key = lax.broadcasted_iota(jnp.int32, s.shape, 0)
            query = lax.broadcasted_iota(jnp.int32, s.shape, 1) // F
            s = jnp.where(key <= query, s, masked_score)
        dp = dot_nn(v, cotts[pair])
        s_buf[where, :] = s
        dp_buf[where, :] = dp
        top = jnp.max(s, axis=0, keepdims=True)
        if diag:
            e = jnp.exp2(s - top)
            l_ref[...] = jnp.sum(e, axis=0, keepdims=True)
            d_ref[...] = jnp.sum(e * dp, axis=0, keepdims=True)
            m_ref[...] = top
        else:
            m_old = m_ref[...]
            m_new = jnp.maximum(m_old, top)
            e = jnp.exp2(s - m_new)
            a = jnp.exp2(m_old - m_new)
            l_ref[...] = l_ref[...] * a + jnp.sum(e, axis=0, keepdims=True)
            d_ref[...] = d_ref[...] * a + jnp.sum(e * dp, axis=0, keepdims=True)
            m_ref[...] = m_new

    def grads(pair, where, k, first=False):
        prob = jnp.exp2(s_buf[where, :] - m_ref[...])
        ds = (prob * (dp_buf[where, :] - d_ref[...])).astype(jnp.bfloat16)
        dv = dot_nn(prob.astype(jnp.bfloat16), cots[pair])
        dk = dot_nn(ds, qs[pair]) * scale
        term = dot_nn(k.T, ds)
        if first:
            dq_acc[pair] = term
        else:
            dq_acc[pair] += term
        return dk, dv

    def grad_copy(j, i):
        return remote(gsend.at[j, i], grecv.at[p, i], g_send.at[j, i], g_recv.at[p, i], at(pp=j))

    def grad_wait(j, i):
        remote(gsend.at[j, i], grecv.at[j, i], g_send.at[j, i], g_recv.at[j, i], at(pp=j)).wait_recv()

    def r1(o):
        dest = peer(g, o, G)
        return remote(ps1.at[dest], pr1.at[g], r1_send.at[dest], r1_recv.at[g], at(gg=dest))

    def r1_wait(o):
        src = peer(g, o, G)
        remote(ps1.at[src], pr1.at[src], r1_send.at[src], r1_recv.at[src], at(gg=src)).wait_recv()

    def r2(o):
        dest = peer(p, o, n)
        return remote(ps2.at[dest], pr2.at[p], r2_send.at[dest], r2_recv.at[p], at(pp=dest))

    def r2_wait(o):
        src = peer(p, o, n)
        remote(ps2.at[src], pr2.at[src], r2_send.at[src], r2_recv.at[src], at(pp=src)).wait_recv()

    pacc[...] = jnp.zeros_like(pacc)

    def one_pair(step, carry):
        i = order(step)
        stats(i, block(p), kv_ref[i, 0], kv_ref[i, 1], True)
        stats(i, prompt_rows, prompt_block(0, i), prompt_block(1, i), False)

        def chunk_stats(o, inner):
            j = p - o
            chunk_wait(j, i)
            stats(i, block(j), kv_all[j, i, 0], kv_all[j, i, 1], False)
            return inner

        lax.fori_loop(1, p + 1, chunk_stats, 0)
        d_ref[...] = d_ref[...] / l_ref[...]
        m_ref[...] = m_ref[...] + jnp.log(l_ref[...]) * log2_e

        h = lax.rem(i, H)
        dk, dv = grads(i, prompt_rows, prompt_block(0, i), True)
        dk = dk.reshape(n, G, piece, E)
        dv = dv.reshape(n, G, piece, E)
        for gg in range(G):
            pacc[gg, :, 0, h] += dk[:, gg]
            pacc[gg, :, 1, h] += dv[:, gg]

        @pl.when(step == pairs - 1)
        def _():
            ps1[...] = pacc[...].astype(jnp.bfloat16)
            for o in range(1, G):
                r1(o).start()

        def chunk_grads(j, inner):
            dk, dv = grads(i, block(j), kv_all[j, i, 0])
            gsend[j, i, 0] = dk.astype(jnp.bfloat16)
            gsend[j, i, 1] = dv.astype(jnp.bfloat16)
            grad_copy(j, i).start()
            return inner

        lax.fori_loop(0, p, chunk_grads, 0)

        @pl.when(step == pairs - 1)
        def _():
            for o in range(1, G):
                r1_wait(o)
            total = pacc[g]
            for o in range(1, G):
                total = total + pr1[peer(g, o, G)].astype(jnp.float32)
            pacc[g] = total
            ps2[...] = total.astype(jnp.bfloat16)
            for o in range(1, n):
                r2(o).start()

        dk, dv = grads(i, block(p), kv_ref[i, 0])
        own[i, 0] = dk
        own[i, 1] = dv
        return carry

    lax.fori_loop(0, pairs, one_pair, 0)

    def write_query_grad(r):
        parts = [dq_acc[r * H + h].T.reshape(L, F, E) for h in range(H)]
        dq_ref[:, r] = (jnp.concatenate(parts, axis=1) * scale).astype(jnp.bfloat16)

    write_query_grad(0)
    for o in range(1, n):
        r2_wait(o)
    total = pacc[g, p]
    for o in range(1, n):
        total = total + pr2[peer(p, o, n)].astype(jnp.float32)
    pg_all[g] = total.astype(jnp.bfloat16)

    def r3(o):
        dest = peer(g, o, G)
        return remote(pg_all.at[g], pg_all.at[g], r3_send.at[dest], r3_recv.at[g], at(gg=dest))

    def r3_wait(o):
        src = peer(g, o, G)
        remote(pg_all.at[src], pg_all.at[src], r3_send.at[src], r3_recv.at[src], at(gg=src)).wait_recv()

    for o in range(1, G):
        r3(o).start()
    for r in range(1, R):
        write_query_grad(r)
    out_copy.start()
    for copy in weight_copies():
        copy.wait()
    for o in range(1, G):
        r3_wait(o)

    def project(tt):
        result = None
        for which in range(2):
            for h in range(H):
                low = pg_all[:, which, h].reshape(G * piece, E)
                term = dot_nt(low, weights[which, tt, :, h * E : (h + 1) * E])
                result = term if result is None else result + term
        return result

    def x_copy(o):
        dest = peer(t, o, T)
        return remote(xs.at[o - 1], xr.at[o - 1], x_send.at[o - 1], x_recv.at[o - 1], at(tt=dest))

    for o in range(1, T):
        xs[o - 1] = project(peer(t, o, T)).astype(jnp.bfloat16)
        x_copy(o).start()
    opart[...] = project(t)

    def add_terms(i, carry):
        def add_one(j, inner):
            grad_wait(j, i)
            own[i] += grecv[j, i].astype(jnp.float32)
            return inner

        return lax.fori_loop(p + 1, n, add_one, carry)

    lax.fori_loop(0, pairs, add_terms, 0)

    result = opart[...]
    for o in range(1, T):
        x_copy(o).wait_recv()
        result = result + xr[o - 1].astype(jnp.float32)
    og[g] = result.astype(jnp.bfloat16)

    def o_copy(o):
        dest = peer(g, o, G)
        return remote(og.at[g], og.at[g], o_send.at[dest], o_recv.at[g], at(gg=dest))

    def o_wait(o):
        src = peer(g, o, G)
        remote(og.at[src], og.at[src], o_send.at[src], o_recv.at[src], at(gg=src)).wait_recv()

    for o in range(1, G):
        o_copy(o).start()
    for which, ref in enumerate((dkey_ref, dvalue_ref)):
        for i in range(pairs):
            wide[which, pl.ds(i, L, stride=pairs), :] = own[i, which]
        ref[...] = wide[which, : L * pairs].astype(jnp.bfloat16)
    for o in range(1, G):
        o_wait(o)
    for gg in range(G):
        out_ref[:, gg * quarter : (gg + 1) * quarter] = og[gg]
    out_copy.wait()

    def pair_sent(i, carry):
        def chunk_sent(j, inner):
            chunk_copy(j, i).wait_send()
            return inner

        def grad_sent(j, inner):
            grad_copy(j, i).wait_send()
            return inner

        lax.fori_loop(p + 1, n, chunk_sent, 0)
        return lax.fori_loop(0, p, grad_sent, carry)

    lax.fori_loop(0, pairs, pair_sent, 0)
    for o in range(1, n):
        prompt_a(o).wait_send()
        r2(o).wait_send()
        for oo in range(1, G):
            prompt_b(o, oo).wait_send()
    for o in range(1, G):
        r1(o).wait_send()
        r3(o).wait_send()
        o_copy(o).wait_send()
    for o in range(1, T):
        x_copy(o).wait_send()


def hand_on(*refs):
    count = 4
    sources, targets, held = refs[:count], refs[count : 2 * count], refs[2 * count : 3 * count]
    in_sem, out_sem = refs[3 * count :]
    arriving = [pltpu.make_async_copy(sources[i], held[i], in_sem.at[i]) for i in range(count)]
    leaving = [pltpu.make_async_copy(held[i], targets[i], out_sem.at[i]) for i in range(count)]
    for copy in arriving:
        copy.start()
    for came, goes in zip(arriving, leaving):
        came.wait()
        goes.start()
    for copy in leaving:
        copy.wait()


def per_device(
    sizes,
    resp_query,
    response_key,
    response_value,
    resp_cotangent,
    prompt_key,
    prompt_value_rows,
    key_matrix,
    value_matrix,
    resp_lengths,
):
    n, G, T = sizes
    L, R, heads, E = resp_query.shape
    H = response_key.shape[2]
    pairs = R * H
    rows = L * heads // H
    prompt_rows = prompt_key.shape[0]
    piece = prompt_rows // G
    width = key_matrix.shape[0]
    quarter = width // T // G
    bf16, f32 = jnp.bfloat16, jnp.float32

    vmem = pl.BlockSpec(memory_space=pltpu.VMEM)
    anywhere = pl.BlockSpec(memory_space=pl.ANY)
    dma = pltpu.SemaphoreType.DMA
    scratch = [
        pltpu.VMEM((L, R, heads, E), bf16),
        pltpu.VMEM((L, R, heads, E), bf16),
        pltpu.VMEM((L, R, heads, E), bf16),
        pltpu.VMEM((2, max(L * pairs, prompt_rows * H), E), f32),
        pltpu.VMEM((pairs, 2, L, E), bf16),
        pltpu.VMEM((G, 2, H, piece, E), bf16),
        pltpu.VMEM((pairs, rows, E), bf16),
        pltpu.VMEM((pairs, rows, E), bf16),
        pltpu.VMEM((pairs, E, rows), bf16),
        pltpu.VMEM((pairs, E, rows), bf16),
        pltpu.VMEM((n, pairs, 2, L, E), bf16),
        pltpu.VMEM((n, G, 2, H, piece, E), bf16),
        pltpu.VMEM((n * L + n * prompt_rows, rows), f32),
        pltpu.VMEM((n * L + n * prompt_rows, rows), f32),
        pltpu.VMEM((1, rows), f32),
        pltpu.VMEM((1, rows), f32),
        pltpu.VMEM((1, rows), f32),
        pltpu.VMEM((pairs, E, rows), f32),
        pltpu.VMEM((pairs, 2, L, E), f32),
        pltpu.VMEM((n, pairs, 2, L, E), bf16),
        pltpu.VMEM((n, pairs, 2, L, E), bf16),
        pltpu.VMEM((G, n, 2, H, piece, E), f32),
        pltpu.VMEM((G, n, 2, H, piece, E), bf16),
        pltpu.VMEM((G, n, 2, H, piece, E), bf16),
        pltpu.VMEM((n, 2, H, piece, E), bf16),
        pltpu.VMEM((n, 2, H, piece, E), bf16),
        pltpu.VMEM((G, 2, H, piece, E), bf16),
        pltpu.VMEM((2, T, quarter, H * E), bf16),
        pltpu.VMEM((prompt_rows, quarter), f32),
        pltpu.VMEM((max(T - 1, 1), prompt_rows, quarter), bf16),
        pltpu.VMEM((max(T - 1, 1), prompt_rows, quarter), bf16),
        pltpu.VMEM((G, prompt_rows, quarter), bf16),
        dma((2, T)),
        dma((3,)),
        dma((n, pairs)),
        dma((n, pairs)),
        dma((n,)),
        dma((n,)),
        dma((G, n)),
        dma((G, n)),
        dma((n, pairs)),
        dma((n, pairs)),
        dma((G,)),
        dma((G,)),
        dma((n,)),
        dma((n,)),
        dma((G,)),
        dma((G,)),
        dma((max(T - 1, 1),)),
        dma((max(T - 1, 1),)),
        dma((G,)),
        dma((G,)),
    ]
    results = pl.pallas_call(
        functools.partial(kernel, sizes),
        out_shape=(
            jax.ShapeDtypeStruct((L, R, heads, E), bf16),
            jax.ShapeDtypeStruct((L * pairs, E), bf16),
            jax.ShapeDtypeStruct((L * pairs, E), bf16),
            jax.ShapeDtypeStruct((prompt_rows, width // T), bf16),
        ),
        in_specs=[pl.BlockSpec(memory_space=pltpu.SMEM)] + [vmem] * 4 + [anywhere] * 4,
        out_specs=(anywhere, vmem, vmem, vmem),
        scratch_shapes=scratch,
        compiler_params=pltpu.CompilerParams(
            collective_id=0, has_side_effects=True, vmem_limit_bytes=60 * 1024 * 1024
        ),
    )(
        resp_lengths,
        response_key.reshape(L * pairs, E),
        response_value.reshape(L * pairs, E),
        prompt_key.reshape(prompt_rows * H, E),
        prompt_value_rows.reshape(prompt_rows * H, E),
        resp_query,
        resp_cotangent,
        key_matrix,
        value_matrix,
    )
    query_grad, key_grad, value_grad, out = pl.pallas_call(
        hand_on,
        out_shape=tuple(jax.ShapeDtypeStruct(x.shape, x.dtype) for x in results),
        in_specs=[anywhere] * 4,
        out_specs=(anywhere,) * 4,
        scratch_shapes=[pltpu.VMEM(x.shape, x.dtype) for x in results] + [dma((4,)), dma((4,))],
        compiler_params=pltpu.CompilerParams(vmem_limit_bytes=60 * 1024 * 1024),
    )(*results)
    shape = response_key.shape
    return (query_grad, key_grad.reshape(shape), value_grad.reshape(shape), out)


def solution(mesh):
    sizes = (mesh.shape["prefix"], mesh.shape["group"], mesh.shape["tensor"])
    placed = (
        P("prefix", "group", "tensor", None),
        P("prefix", "group", "tensor", None),
        P("prefix", "group", "tensor", None),
        P("prefix", "group", "tensor", None),
        P("prefix", "tensor", None),
        P("prefix", "tensor", None),
        P(None, "tensor"),
        P(None, "tensor"),
        P(),
    )
    return jax.shard_map(
        functools.partial(per_device, sizes),
        mesh=mesh,
        in_specs=placed,
        out_specs=(
            P("prefix", "group", "tensor", None),
            P("prefix", "group", "tensor", None),
            P("prefix", "group", "tensor", None),
            P("prefix", "tensor"),
        ),
        check_vma=False,
    )
```

```python
import functools
import math

import jax
import jax.numpy as jnp
from jax import lax
from jax.experimental import pallas as pl
from jax.experimental.pallas import tpu as pltpu
from jax.sharding import PartitionSpec as P

MESH = pl.DeviceIdType.MESH
masked_score = -1e30
log2_e = math.log2(math.e)


def dot_nt(a, b):
    return lax.dot_general(a, b, (((1,), (1,)), ((), ())), preferred_element_type=jnp.float32)


def dot_nn(a, b):
    return lax.dot_general(a, b, (((1,), (0,)), ((), ())), preferred_element_type=jnp.float32)


def kernel(
    sizes,
    len_ref,
    key_ref,
    value_ref,
    pkey_ref,
    pvalue_ref,
    q_hbm,
    cot_hbm,
    km_ref,
    vm_ref,
    dq_hbm,
    dkey_ref,
    dvalue_ref,
    out_ref,
    q_ref,
    cot_ref,
    dq_ref,
    wide,
    kv_ref,
    pr_ref,
    qs,
    cots,
    qts,
    cotts,
    kv_all,
    pr_all,
    s_buf,
    dp_buf,
    m_ref,
    l_ref,
    d_ref,
    dq_acc,
    own,
    gsend,
    grecv,
    pacc,
    ps1,
    pr1,
    ps2,
    pr2,
    pg_all,
    weights,
    opart,
    xs,
    xr,
    og,
    w_sem,
    q_sem,
    c_send,
    c_recv,
    a_send,
    a_recv,
    b_send,
    b_recv,
    g_send,
    g_recv,
    r1_send,
    r1_recv,
    r2_send,
    r2_recv,
    r3_send,
    r3_recv,
    x_send,
    x_recv,
    o_send,
    o_recv,
):
    n, G, T = sizes
    p = lax.axis_index("prefix")
    g = lax.axis_index("group")
    t = lax.axis_index("tensor")
    L, R, heads, E = q_ref.shape
    pairs = kv_ref.shape[0]
    H = pairs // R
    F = heads // H
    rows = L * F
    piece = pr_ref.shape[3]
    quarter = weights.shape[2]
    scale = 1.0 / math.sqrt(E)
    log_scale = scale * log2_e

    def at(pp=None, gg=None, tt=None):
        return (p if pp is None else pp, g if gg is None else gg, t if tt is None else tt)

    def peer(me, o, size):
        return lax.rem(me + o, size)

    def remote(src, dst, send, recv, where):
        return pltpu.make_async_remote_copy(
            src_ref=src, dst_ref=dst, send_sem=send, recv_sem=recv, device_id=where, device_id_type=MESH
        )

    barrier = pltpu.get_barrier_semaphore()
    for o in range(1, n):
        pl.semaphore_signal(barrier, inc=1, device_id=at(pp=peer(p, o, n)), device_id_type=MESH)
    for o in range(1, G):
        pl.semaphore_signal(barrier, inc=1, device_id=at(gg=peer(g, o, G)), device_id_type=MESH)
    for o in range(1, T):
        pl.semaphore_signal(barrier, inc=1, device_id=at(tt=peer(t, o, T)), device_id_type=MESH)

    half = quarter * G

    def weight_copies():
        copies = []
        for which, ref in enumerate((km_ref, vm_ref)):
            for tt in range(T):
                start = pl.multiple_of(tt * half + g * quarter, 16)
                copies.append(
                    pltpu.make_async_copy(
                        ref.at[pl.ds(start, quarter)], weights.at[which, tt], w_sem.at[which, tt]
                    )
                )
        return copies

    in_copies = (
        pltpu.make_async_copy(q_hbm, q_ref, q_sem.at[0]),
        pltpu.make_async_copy(cot_hbm, cot_ref, q_sem.at[1]),
    )
    out_copy = pltpu.make_async_copy(dq_ref, dq_hbm, q_sem.at[2])
    for copy in in_copies:
        copy.start()
    for copy in weight_copies():
        copy.start()

    for which, ref in enumerate((key_ref, value_ref)):
        wide[which, : L * pairs] = ref[...].astype(jnp.float32)
        for i in range(pairs):
            kv_ref[i, which] = wide[which, pl.ds(i, L, stride=pairs), :].astype(jnp.bfloat16)
    for which, ref in enumerate((pkey_ref, pvalue_ref)):
        wide[which, : G * piece * H] = ref[...].astype(jnp.float32)
        for gg in range(G):
            for h in range(H):
                rows_of = pl.ds(gg * piece * H + h, piece, stride=H)
                pr_ref[gg, which, h] = wide[which, rows_of, :].astype(jnp.bfloat16)

    pl.semaphore_wait(barrier, n + G + T - 3)

    def order(k):
        return lax.rem(k, R) * H + k // R

    up, down = lax.rem(p + 1, n), lax.rem(p + n - 1, n)

    def chunk_copy(src, j, i):
        return remote(src, kv_all.at[j, i], c_send.at[j, i], c_recv.at[j, i], at(pp=up))

    def chunk_wait(j, i):
        chunk_copy(kv_ref.at[i], j, i).wait_recv()

    def send_own(k):
        @pl.when((p < n - 1) & (k < pairs))
        def _():
            i = order(k)
            chunk_copy(kv_ref.at[i], p, i).start()

    def pass_on(k):
        @pl.when((p < n - 1) & (k < pairs))
        def _():
            i = order(k)

            def one(o, inner):
                chunk_wait(p - o, i)
                chunk_copy(kv_all.at[p - o, i], p - o, i).start()
                return inner

            lax.fori_loop(1, p + 1, one, 0)

    def prompt_a(o):
        dest = peer(p, o, n)
        return remote(pr_ref.at[g], pr_all.at[p, g], a_send.at[dest], a_recv.at[p], at(pp=dest))

    def prompt_a_wait(o):
        src = peer(p, o, n)
        remote(pr_ref.at[g], pr_all.at[src, g], a_send.at[src], a_recv.at[src], at(pp=src)).wait_recv()

    for o in range(1, n):
        prompt_a(o).start()

    send_own(0)
    send_own(1)

    def prompt_b(o, oo):
        src, dest = peer(p, o, n), peer(g, oo, G)
        return remote(
            pr_all.at[src, g], pr_all.at[src, g], b_send.at[dest, src], b_recv.at[g, src], at(gg=dest)
        )

    def prompt_b_wait(o, oo):
        src, frm = peer(p, o, n), peer(g, oo, G)
        remote(
            pr_all.at[src, frm], pr_all.at[src, frm], b_send.at[frm, src], b_recv.at[frm, src], at(gg=frm)
        ).wait_recv()

    pr_all[p] = pr_ref[...]
    pos = p * L + lax.broadcasted_iota(jnp.int32, (L, F, E), 0)
    for copy in in_copies:
        copy.wait()
    for r in range(R):
        length = len_ref[g * R + r]
        q = q_ref[:, r].astype(jnp.float32)
        c = cot_ref[:, r].astype(jnp.float32)
        for h in range(H):
            part = q[:, h * F : (h + 1) * F].reshape(rows, E)
            qs[r * H + h] = part.astype(jnp.bfloat16)
            qts[r * H + h] = part.T.astype(jnp.bfloat16)
            live = jnp.where(pos < length, c[:, h * F : (h + 1) * F], 0.0).reshape(rows, E)
            cots[r * H + h] = live.astype(jnp.bfloat16)
            cotts[r * H + h] = live.T.astype(jnp.bfloat16)
        if r == 0:
            for o in range(1, n):
                prompt_a_wait(o)
                for oo in range(1, G):
                    prompt_b(o, oo).start()
    for o in range(1, n):
        for oo in range(1, G):
            prompt_b_wait(o, oo)

    prompt_keys = n * G * piece

    def prompt_block(which, pair):
        return pr_all[:, :, which, lax.rem(pair, H)].reshape(prompt_keys, E)

    def block(j):
        return pl.ds(pl.multiple_of(j * L, L), L)

    prompt_rows = pl.ds(n * L, prompt_keys)

    def stats(pair, where, k, v, diag):
        s = dot_nn(k, qts[pair]) * log_scale
        if diag:
            key = lax.broadcasted_iota(jnp.int32, s.shape, 0)
            query = lax.broadcasted_iota(jnp.int32, s.shape, 1) // F
            s = jnp.where(key <= query, s, masked_score)
        dp = dot_nn(v, cotts[pair])
        s_buf[where, :] = s
        dp_buf[where, :] = dp
        top = jnp.max(s, axis=0, keepdims=True)
        if diag:
            e = jnp.exp2(s - top)
            l_ref[...] = jnp.sum(e, axis=0, keepdims=True)
            d_ref[...] = jnp.sum(e * dp, axis=0, keepdims=True)
            m_ref[...] = top
        else:
            m_old = m_ref[...]
            m_new = jnp.maximum(m_old, top)
            e = jnp.exp2(s - m_new)
            a = jnp.exp2(m_old - m_new)
            l_ref[...] = l_ref[...] * a + jnp.sum(e, axis=0, keepdims=True)
            d_ref[...] = d_ref[...] * a + jnp.sum(e * dp, axis=0, keepdims=True)
            m_ref[...] = m_new

    def grads(pair, where, k, first=False):
        prob = jnp.exp2(s_buf[where, :] - m_ref[...])
        ds = (prob * (dp_buf[where, :] - d_ref[...])).astype(jnp.bfloat16)
        dv = dot_nn(prob.astype(jnp.bfloat16), cots[pair])
        dk = dot_nn(ds, qs[pair]) * scale
        term = dot_nn(k.T, ds)
        if first:
            dq_acc[pair] = term
        else:
            dq_acc[pair] += term
        return dk, dv

    def grad_copy(j, i):
        return remote(gsend.at[j, i], grecv.at[j, i], g_send.at[j, i], g_recv.at[j, i], at(pp=down))

    def add_up(k):
        i = order(k)

        def one(j, inner):
            grad_copy(j, i).wait_recv()
            total = gsend[j, i].astype(jnp.float32) + grecv[j, i].astype(jnp.float32)
            gsend[j, i] = total.astype(jnp.bfloat16)
            grad_copy(j, i).start()
            return inner

        lax.fori_loop(0, p, one, 0)
        grad_copy(p, i).wait_recv()
        own[i] += grecv[p, i].astype(jnp.float32)

    lag = n - 1 - p

    def r1(o):
        dest = peer(g, o, G)
        return remote(ps1.at[dest], pr1.at[g], r1_send.at[dest], r1_recv.at[g], at(gg=dest))

    def r1_wait(o):
        src = peer(g, o, G)
        remote(ps1.at[src], pr1.at[src], r1_send.at[src], r1_recv.at[src], at(gg=src)).wait_recv()

    def r2(o):
        dest = peer(p, o, n)
        return remote(ps2.at[dest], pr2.at[p], r2_send.at[dest], r2_recv.at[p], at(pp=dest))

    def r2_wait(o):
        src = peer(p, o, n)
        remote(ps2.at[src], pr2.at[src], r2_send.at[src], r2_recv.at[src], at(pp=src)).wait_recv()

    pacc[...] = jnp.zeros_like(pacc)

    def one_pair(step, carry):
        i = order(step)

        @pl.when(step == 0)
        def _():
            pass_on(0)

        pass_on(step + 1)
        send_own(step + 2)
        stats(i, block(p), kv_ref[i, 0], kv_ref[i, 1], True)
        stats(i, prompt_rows, prompt_block(0, i), prompt_block(1, i), False)

        def chunk_stats(o, inner):
            j = p - o

            @pl.when(p == n - 1)
            def _():
                chunk_wait(j, i)

            stats(i, block(j), kv_all[j, i, 0], kv_all[j, i, 1], False)
            return inner

        lax.fori_loop(1, p + 1, chunk_stats, 0)
        d_ref[...] = d_ref[...] / l_ref[...]
        m_ref[...] = m_ref[...] + jnp.log(l_ref[...]) * log2_e

        h = lax.rem(i, H)
        dk, dv = grads(i, prompt_rows, prompt_block(0, i), True)
        dk = dk.reshape(n, G, piece, E)
        dv = dv.reshape(n, G, piece, E)
        for gg in range(G):
            pacc[gg, :, 0, h] += dk[:, gg]
            pacc[gg, :, 1, h] += dv[:, gg]

        @pl.when(step == pairs - 1)
        def _():
            ps1[...] = pacc[...].astype(jnp.bfloat16)
            for o in range(1, G):
                r1(o).start()

        def chunk_grads(j, inner):
            dk, dv = grads(i, block(j), kv_all[j, i, 0])
            gsend[j, i, 0] = dk.astype(jnp.bfloat16)
            gsend[j, i, 1] = dv.astype(jnp.bfloat16)

            @pl.when(p == n - 1)
            def _():
                grad_copy(j, i).start()

            return inner

        lax.fori_loop(0, p, chunk_grads, 0)

        @pl.when(step == pairs - 1)
        def _():
            for o in range(1, G):
                r1_wait(o)
            total = pacc[g]
            for o in range(1, G):
                total = total + pr1[peer(g, o, G)].astype(jnp.float32)
            pacc[g] = total
            ps2[...] = total.astype(jnp.bfloat16)
            for o in range(1, n):
                r2(o).start()

        dk, dv = grads(i, block(p), kv_ref[i, 0])
        own[i, 0] = dk
        own[i, 1] = dv

        @pl.when((lag > 0) & (step >= lag))
        def _():
            add_up(step - lag)

        return carry

    lax.fori_loop(0, pairs, one_pair, 0)

    def write_query_grad(r):
        parts = [dq_acc[r * H + h].T.reshape(L, F, E) for h in range(H)]
        dq_ref[:, r] = (jnp.concatenate(parts, axis=1) * scale).astype(jnp.bfloat16)

    def add_rest(k, carry):
        add_up(k)
        return carry

    left = jnp.maximum(pairs - lag, 0)

    for o in range(1, n):
        r2_wait(o)
    total = pacc[g, p]
    for o in range(1, n):
        total = total + pr2[peer(p, o, n)].astype(jnp.float32)
    pg_all[g] = total.astype(jnp.bfloat16)

    def r3(o):
        dest = peer(g, o, G)
        return remote(pg_all.at[g], pg_all.at[g], r3_send.at[dest], r3_recv.at[g], at(gg=dest))

    def r3_wait(o):
        src = peer(g, o, G)
        remote(pg_all.at[src], pg_all.at[src], r3_send.at[src], r3_recv.at[src], at(gg=src)).wait_recv()

    for o in range(1, G):
        r3(o).start()
    lax.fori_loop(left, jnp.where(p > 0, pairs, left), add_rest, 0)
    for r in range(R):
        write_query_grad(r)
    out_copy.start()
    for copy in weight_copies():
        copy.wait()
    for o in range(1, G):
        r3_wait(o)

    def project(tt):
        result = None
        for which in range(2):
            for h in range(H):
                low = pg_all[:, which, h].reshape(G * piece, E)
                term = dot_nt(low, weights[which, tt, :, h * E : (h + 1) * E])
                result = term if result is None else result + term
        return result

    def x_copy(o):
        dest = peer(t, o, T)
        return remote(xs.at[o - 1], xr.at[o - 1], x_send.at[o - 1], x_recv.at[o - 1], at(tt=dest))

    for o in range(1, T):
        xs[o - 1] = project(peer(t, o, T)).astype(jnp.bfloat16)
        x_copy(o).start()
    opart[...] = project(t)

    result = opart[...]
    for o in range(1, T):
        x_copy(o).wait_recv()
        result = result + xr[o - 1].astype(jnp.float32)
    og[g] = result.astype(jnp.bfloat16)

    def o_copy(o):
        dest = peer(g, o, G)
        return remote(og.at[g], og.at[g], o_send.at[dest], o_recv.at[g], at(gg=dest))

    def o_wait(o):
        src = peer(g, o, G)
        remote(og.at[src], og.at[src], o_send.at[src], o_recv.at[src], at(gg=src)).wait_recv()

    for o in range(1, G):
        o_copy(o).start()
    lax.fori_loop(left, jnp.where(p > 0, left, pairs), add_rest, 0)
    for which, ref in enumerate((dkey_ref, dvalue_ref)):
        for i in range(pairs):
            wide[which, pl.ds(i, L, stride=pairs), :] = own[i, which]
        ref[...] = wide[which, : L * pairs].astype(jnp.bfloat16)
    for o in range(1, G):
        o_wait(o)
    for gg in range(G):
        out_ref[:, gg * quarter : (gg + 1) * quarter] = og[gg]
    out_copy.wait()

    def pair_sent(i, carry):
        def chunk_sent(j, inner):
            chunk_copy(kv_ref.at[i], j, i).wait_send()
            return inner

        def grad_sent(j, inner):
            grad_copy(j, i).wait_send()
            return inner

        lax.fori_loop(0, jnp.where(p < n - 1, p + 1, 0), chunk_sent, 0)
        return lax.fori_loop(0, p, grad_sent, carry)

    lax.fori_loop(0, pairs, pair_sent, 0)
    for o in range(1, n):
        prompt_a(o).wait_send()
        r2(o).wait_send()
        for oo in range(1, G):
            prompt_b(o, oo).wait_send()
    for o in range(1, G):
        r1(o).wait_send()
        r3(o).wait_send()
        o_copy(o).wait_send()
    for o in range(1, T):
        x_copy(o).wait_send()


def hand_on(*refs):
    count = 4
    sources, targets, held = refs[:count], refs[count : 2 * count], refs[2 * count : 3 * count]
    in_sem, out_sem = refs[3 * count :]
    arriving = [pltpu.make_async_copy(sources[i], held[i], in_sem.at[i]) for i in range(count)]
    leaving = [pltpu.make_async_copy(held[i], targets[i], out_sem.at[i]) for i in range(count)]
    for copy in arriving:
        copy.start()
    for came, goes in zip(arriving, leaving):
        came.wait()
        goes.start()
    for copy in leaving:
        copy.wait()


def per_device(
    sizes,
    resp_query,
    response_key,
    response_value,
    resp_cotangent,
    prompt_key,
    prompt_value_rows,
    key_matrix,
    value_matrix,
    resp_lengths,
):
    n, G, T = sizes
    L, R, heads, E = resp_query.shape
    H = response_key.shape[2]
    pairs = R * H
    rows = L * heads // H
    prompt_rows = prompt_key.shape[0]
    piece = prompt_rows // G
    width = key_matrix.shape[0]
    quarter = width // T // G
    bf16, f32 = jnp.bfloat16, jnp.float32

    vmem = pl.BlockSpec(memory_space=pltpu.VMEM)
    anywhere = pl.BlockSpec(memory_space=pl.ANY)
    dma = pltpu.SemaphoreType.DMA
    scratch = [
        pltpu.VMEM((L, R, heads, E), bf16),
        pltpu.VMEM((L, R, heads, E), bf16),
        pltpu.VMEM((L, R, heads, E), bf16),
        pltpu.VMEM((2, max(L * pairs, prompt_rows * H), E), f32),
        pltpu.VMEM((pairs, 2, L, E), bf16),
        pltpu.VMEM((G, 2, H, piece, E), bf16),
        pltpu.VMEM((pairs, rows, E), bf16),
        pltpu.VMEM((pairs, rows, E), bf16),
        pltpu.VMEM((pairs, E, rows), bf16),
        pltpu.VMEM((pairs, E, rows), bf16),
        pltpu.VMEM((n, pairs, 2, L, E), bf16),
        pltpu.VMEM((n, G, 2, H, piece, E), bf16),
        pltpu.VMEM((n * L + n * prompt_rows, rows), f32),
        pltpu.VMEM((n * L + n * prompt_rows, rows), f32),
        pltpu.VMEM((1, rows), f32),
        pltpu.VMEM((1, rows), f32),
        pltpu.VMEM((1, rows), f32),
        pltpu.VMEM((pairs, E, rows), f32),
        pltpu.VMEM((pairs, 2, L, E), f32),
        pltpu.VMEM((n, pairs, 2, L, E), bf16),
        pltpu.VMEM((n, pairs, 2, L, E), bf16),
        pltpu.VMEM((G, n, 2, H, piece, E), f32),
        pltpu.VMEM((G, n, 2, H, piece, E), bf16),
        pltpu.VMEM((G, n, 2, H, piece, E), bf16),
        pltpu.VMEM((n, 2, H, piece, E), bf16),
        pltpu.VMEM((n, 2, H, piece, E), bf16),
        pltpu.VMEM((G, 2, H, piece, E), bf16),
        pltpu.VMEM((2, T, quarter, H * E), bf16),
        pltpu.VMEM((prompt_rows, quarter), f32),
        pltpu.VMEM((max(T - 1, 1), prompt_rows, quarter), bf16),
        pltpu.VMEM((max(T - 1, 1), prompt_rows, quarter), bf16),
        pltpu.VMEM((G, prompt_rows, quarter), bf16),
        dma((2, T)),
        dma((3,)),
        dma((n, pairs)),
        dma((n, pairs)),
        dma((n,)),
        dma((n,)),
        dma((G, n)),
        dma((G, n)),
        dma((n, pairs)),
        dma((n, pairs)),
        dma((G,)),
        dma((G,)),
        dma((n,)),
        dma((n,)),
        dma((G,)),
        dma((G,)),
        dma((max(T - 1, 1),)),
        dma((max(T - 1, 1),)),
        dma((G,)),
        dma((G,)),
    ]
    results = pl.pallas_call(
        functools.partial(kernel, sizes),
        out_shape=(
            jax.ShapeDtypeStruct((L, R, heads, E), bf16),
            jax.ShapeDtypeStruct((L * pairs, E), bf16),
            jax.ShapeDtypeStruct((L * pairs, E), bf16),
            jax.ShapeDtypeStruct((prompt_rows, width // T), bf16),
        ),
        in_specs=[pl.BlockSpec(memory_space=pltpu.SMEM)] + [vmem] * 4 + [anywhere] * 4,
        out_specs=(anywhere, vmem, vmem, vmem),
        scratch_shapes=scratch,
        compiler_params=pltpu.CompilerParams(
            collective_id=0, has_side_effects=True, vmem_limit_bytes=60 * 1024 * 1024
        ),
    )(
        resp_lengths,
        response_key.reshape(L * pairs, E),
        response_value.reshape(L * pairs, E),
        prompt_key.reshape(prompt_rows * H, E),
        prompt_value_rows.reshape(prompt_rows * H, E),
        resp_query,
        resp_cotangent,
        key_matrix,
        value_matrix,
    )
    query_grad, key_grad, value_grad, out = pl.pallas_call(
        hand_on,
        out_shape=tuple(jax.ShapeDtypeStruct(x.shape, x.dtype) for x in results),
        in_specs=[anywhere] * 4,
        out_specs=(anywhere,) * 4,
        scratch_shapes=[pltpu.VMEM(x.shape, x.dtype) for x in results] + [dma((4,)), dma((4,))],
        compiler_params=pltpu.CompilerParams(vmem_limit_bytes=60 * 1024 * 1024),
    )(*results)
    shape = response_key.shape
    return (query_grad, key_grad.reshape(shape), value_grad.reshape(shape), out)


def solution(mesh):
    sizes = (mesh.shape["prefix"], mesh.shape["group"], mesh.shape["tensor"])
    placed = (
        P("prefix", "group", "tensor", None),
        P("prefix", "group", "tensor", None),
        P("prefix", "group", "tensor", None),
        P("prefix", "group", "tensor", None),
        P("prefix", "tensor", None),
        P("prefix", "tensor", None),
        P(None, "tensor"),
        P(None, "tensor"),
        P(),
    )
    return jax.shard_map(
        functools.partial(per_device, sizes),
        mesh=mesh,
        in_specs=placed,
        out_specs=(
            P("prefix", "group", "tensor", None),
            P("prefix", "group", "tensor", None),
            P("prefix", "group", "tensor", None),
            P("prefix", "tensor"),
        ),
        check_vma=False,
    )
```

```python
import functools
import math

import jax
import jax.numpy as jnp
from jax import lax
from jax.experimental import pallas as pl
from jax.experimental.pallas import tpu as pltpu
from jax.sharding import PartitionSpec as P

MESH = pl.DeviceIdType.MESH
masked_score = -1e30
log2_e = math.log2(math.e)


def dot_nt(a, b):
    return lax.dot_general(a, b, (((1,), (1,)), ((), ())), preferred_element_type=jnp.float32)


def dot_nn(a, b):
    return lax.dot_general(a, b, (((1,), (0,)), ((), ())), preferred_element_type=jnp.float32)


def kernel(
    sizes,
    len_ref,
    key_ref,
    value_ref,
    pkey_ref,
    pvalue_ref,
    q_hbm,
    cot_hbm,
    km_ref,
    vm_ref,
    dq_hbm,
    dkey_ref,
    dvalue_ref,
    out_ref,
    q_ref,
    cot_ref,
    dq_ref,
    wide,
    kv_ref,
    pr_ref,
    qs,
    cots,
    qts,
    cotts,
    kv_all,
    pr_all,
    kcat,
    vcat,
    kcat_t,
    dk_acc,
    dv_acc,
    dq_acc,
    own,
    gsend,
    grecv,
    pacc,
    ps1,
    pr1,
    ps2,
    pr2,
    pg_all,
    weights,
    opart,
    xs,
    xr,
    og,
    w_sem,
    q_sem,
    c_send,
    c_recv,
    a_send,
    a_recv,
    b_send,
    b_recv,
    g_send,
    g_recv,
    r1_send,
    r1_recv,
    r2_send,
    r2_recv,
    r3_send,
    r3_recv,
    x_send,
    x_recv,
    o_send,
    o_recv,
):
    n, G, T = sizes
    p = lax.axis_index("prefix")
    g = lax.axis_index("group")
    t = lax.axis_index("tensor")
    L, R, heads, E = q_ref.shape
    pairs = kv_ref.shape[0]
    H = pairs // R
    F = heads // H
    rows = L * F
    piece = pr_ref.shape[3]
    quarter = weights.shape[2]
    scale = 1.0 / math.sqrt(E)
    log_scale = scale * log2_e

    def at(pp=None, gg=None, tt=None):
        return (p if pp is None else pp, g if gg is None else gg, t if tt is None else tt)

    def peer(me, o, size):
        return lax.rem(me + o, size)

    def remote(src, dst, send, recv, where):
        return pltpu.make_async_remote_copy(
            src_ref=src, dst_ref=dst, send_sem=send, recv_sem=recv, device_id=where, device_id_type=MESH
        )

    barrier = pltpu.get_barrier_semaphore()
    for o in range(1, n):
        pl.semaphore_signal(barrier, inc=1, device_id=at(pp=peer(p, o, n)), device_id_type=MESH)
    for o in range(1, G):
        pl.semaphore_signal(barrier, inc=1, device_id=at(gg=peer(g, o, G)), device_id_type=MESH)
    for o in range(1, T):
        pl.semaphore_signal(barrier, inc=1, device_id=at(tt=peer(t, o, T)), device_id_type=MESH)

    half = quarter * G

    def weight_copies():
        copies = []
        for which, ref in enumerate((km_ref, vm_ref)):
            for tt in range(T):
                start = pl.multiple_of(tt * half + g * quarter, 16)
                copies.append(
                    pltpu.make_async_copy(
                        ref.at[pl.ds(start, quarter)], weights.at[which, tt], w_sem.at[which, tt]
                    )
                )
        return copies

    in_copies = (
        pltpu.make_async_copy(q_hbm, q_ref, q_sem.at[0]),
        pltpu.make_async_copy(cot_hbm, cot_ref, q_sem.at[1]),
    )
    out_copy = pltpu.make_async_copy(dq_ref, dq_hbm, q_sem.at[2])
    for copy in in_copies:
        copy.start()
    for copy in weight_copies():
        copy.start()

    for which, ref in enumerate((key_ref, value_ref)):
        wide[which, : L * pairs] = ref[...].astype(jnp.float32)
        for i in range(pairs):
            kv_ref[i, which] = wide[which, pl.ds(i, L, stride=pairs), :].astype(jnp.bfloat16)
    for which, ref in enumerate((pkey_ref, pvalue_ref)):
        wide[which, : G * piece * H] = ref[...].astype(jnp.float32)
        for gg in range(G):
            for h in range(H):
                rows_of = pl.ds(gg * piece * H + h, piece, stride=H)
                pr_ref[gg, which, h] = wide[which, rows_of, :].astype(jnp.bfloat16)

    pl.semaphore_wait(barrier, n + G + T - 3)

    def order(k):
        return lax.rem(k, R) * H + k // R

    up, down = lax.rem(p + 1, n), lax.rem(p + n - 1, n)

    def chunk_copy(src, j, i):
        return remote(src, kv_all.at[j, i], c_send.at[j, i], c_recv.at[j, i], at(pp=up))

    def chunk_wait(j, i):
        chunk_copy(kv_ref.at[i], j, i).wait_recv()

    def send_own(k):
        @pl.when((p < n - 1) & (k < pairs))
        def _():
            i = order(k)
            chunk_copy(kv_ref.at[i], p, i).start()

    def pass_on(k):
        @pl.when((p < n - 1) & (k < pairs))
        def _():
            i = order(k)

            def one(o, inner):
                chunk_wait(p - o, i)
                chunk_copy(kv_all.at[p - o, i], p - o, i).start()
                return inner

            lax.fori_loop(1, p + 1, one, 0)

    def prompt_a(o):
        dest = peer(p, o, n)
        return remote(pr_ref.at[g], pr_all.at[p, g], a_send.at[dest], a_recv.at[p], at(pp=dest))

    def prompt_a_wait(o):
        src = peer(p, o, n)
        remote(pr_ref.at[g], pr_all.at[src, g], a_send.at[src], a_recv.at[src], at(pp=src)).wait_recv()

    for o in range(1, n):
        prompt_a(o).start()

    send_own(0)
    send_own(1)

    def prompt_b(o, oo):
        src, dest = peer(p, o, n), peer(g, oo, G)
        return remote(
            pr_all.at[src, g], pr_all.at[src, g], b_send.at[dest, src], b_recv.at[g, src], at(gg=dest)
        )

    def prompt_b_wait(o, oo):
        src, frm = peer(p, o, n), peer(g, oo, G)
        remote(
            pr_all.at[src, frm], pr_all.at[src, frm], b_send.at[frm, src], b_recv.at[frm, src], at(gg=frm)
        ).wait_recv()

    pr_all[p] = pr_ref[...]
    pos = p * L + lax.broadcasted_iota(jnp.int32, (L, F, E), 0)
    for copy in in_copies:
        copy.wait()
    for r in range(R):
        length = len_ref[g * R + r]
        q = q_ref[:, r].astype(jnp.float32)
        c = cot_ref[:, r].astype(jnp.float32)
        for h in range(H):
            part = q[:, h * F : (h + 1) * F].reshape(rows, E)
            qs[r * H + h] = part.astype(jnp.bfloat16)
            qts[r * H + h] = part.T.astype(jnp.bfloat16)
            live = jnp.where(pos < length, c[:, h * F : (h + 1) * F], 0.0).reshape(rows, E)
            cots[r * H + h] = live.astype(jnp.bfloat16)
            cotts[r * H + h] = live.T.astype(jnp.bfloat16)
        if r == 0:
            for o in range(1, n):
                prompt_a_wait(o)
                for oo in range(1, G):
                    prompt_b(o, oo).start()
    for o in range(1, n):
        for oo in range(1, G):
            prompt_b_wait(o, oo)

    prompt_keys = n * G * piece

    def prompt_block(which, pair):
        return pr_all[:, :, which, lax.rem(pair, H)].reshape(prompt_keys, E)

    def block(j):
        return pl.ds(pl.multiple_of(prompt_keys + j * L, L), L)

    wide_rows = 256 if rows % 512 == 0 else rows
    abreast = 2 if rows % 512 == 0 else 1

    def query_block(i, c, b, keys):
        cols = pl.ds(pl.multiple_of(b * wide_rows, wide_rows), wide_rows)
        q_t, cot_t = qts[i, :, cols], cotts[i, :, cols]
        s = dot_nn(kcat[:keys], q_t) * log_scale
        key = lax.broadcasted_iota(jnp.int32, (L, wide_rows), 0)
        query = (lax.broadcasted_iota(jnp.int32, (L, wide_rows), 1) + b * wide_rows) // F
        last = jnp.where(key <= query, s[keys - L :], masked_score)
        s = jnp.concatenate([s[: keys - L], last], axis=0)
        e = jnp.exp2(s - jnp.max(s, axis=0, keepdims=True))
        inverse = 1.0 / jnp.sum(e, axis=0, keepdims=True)
        dp = dot_nn(vcat[:keys], cot_t)
        prob = e * inverse
        weighted = prob * dp
        delta = jnp.sum(weighted, axis=0, keepdims=True)
        ds = (weighted - prob * delta).astype(jnp.bfloat16)
        dv = dot_nn(prob.astype(jnp.bfloat16), cots[i, cols])
        dk = dot_nn(ds, qs[i, cols])
        dq_acc[i, :, cols] = dot_nn(kcat_t[:, :keys], ds)
        return dk, dv

    def whole_pair(i, c):
        keys = prompt_keys + (c + 1) * L
        kcat_t[:, :keys] = kcat[:keys].T
        dk_acc[:keys] = jnp.zeros((keys, E), jnp.float32)
        dv_acc[:keys] = jnp.zeros((keys, E), jnp.float32)

        def some(b, carry):
            terms = [query_block(i, c, b * abreast + k, keys) for k in range(abreast)]
            dk_acc[:keys] += functools.reduce(lambda x, y: x + y, [x[0] for x in terms])
            dv_acc[:keys] += functools.reduce(lambda x, y: x + y, [x[1] for x in terms])
            return carry

        lax.fori_loop(0, rows // (wide_rows * abreast), some, 0)

    def grad_copy(j, i):
        return remote(gsend.at[j, i], grecv.at[j, i], g_send.at[j, i], g_recv.at[j, i], at(pp=down))

    def add_up(k):
        i = order(k)

        def one(j, inner):
            grad_copy(j, i).wait_recv()
            total = gsend[j, i].astype(jnp.float32) + grecv[j, i].astype(jnp.float32)
            gsend[j, i] = total.astype(jnp.bfloat16)
            grad_copy(j, i).start()
            return inner

        lax.fori_loop(0, p, one, 0)
        grad_copy(p, i).wait_recv()
        own[i] += grecv[p, i].astype(jnp.float32)

    lag = n - 1 - p

    def r1(o):
        dest = peer(g, o, G)
        return remote(ps1.at[dest], pr1.at[g], r1_send.at[dest], r1_recv.at[g], at(gg=dest))

    def r1_wait(o):
        src = peer(g, o, G)
        remote(ps1.at[src], pr1.at[src], r1_send.at[src], r1_recv.at[src], at(gg=src)).wait_recv()

    def r2(o):
        dest = peer(p, o, n)
        return remote(ps2.at[dest], pr2.at[p], r2_send.at[dest], r2_recv.at[p], at(pp=dest))

    def r2_wait(o):
        src = peer(p, o, n)
        remote(ps2.at[src], pr2.at[src], r2_send.at[src], r2_recv.at[src], at(pp=src)).wait_recv()

    pacc[...] = jnp.zeros_like(pacc)

    def one_pair(step, carry):
        i = order(step)

        @pl.when(step == 0)
        def _():
            pass_on(0)

        pass_on(step + 1)
        send_own(step + 2)
        kcat[:prompt_keys] = prompt_block(0, i)
        vcat[:prompt_keys] = prompt_block(1, i)
        kcat[block(p), :] = kv_ref[i, 0]
        vcat[block(p), :] = kv_ref[i, 1]

        def place(o, inner):
            j = p - o

            @pl.when(p == n - 1)
            def _():
                chunk_wait(j, i)

            kcat[block(j), :] = kv_all[j, i, 0]
            vcat[block(j), :] = kv_all[j, i, 1]
            return inner

        lax.fori_loop(1, p + 1, place, 0)
        for c in range(n):

            @pl.when(p == c)
            def _():
                whole_pair(i, c)

        h = lax.rem(i, H)
        dk = (dk_acc[:prompt_keys] * scale).reshape(n, G, piece, E)
        dv = dv_acc[:prompt_keys].reshape(n, G, piece, E)
        for gg in range(G):
            pacc[gg, :, 0, h] += dk[:, gg]
            pacc[gg, :, 1, h] += dv[:, gg]

        @pl.when(step == pairs - 1)
        def _():
            ps1[...] = pacc[...].astype(jnp.bfloat16)
            for o in range(1, G):
                r1(o).start()

        def chunk_grads(j, inner):
            gsend[j, i, 0] = (dk_acc[block(j), :] * scale).astype(jnp.bfloat16)
            gsend[j, i, 1] = dv_acc[block(j), :].astype(jnp.bfloat16)

            @pl.when(p == n - 1)
            def _():
                grad_copy(j, i).start()

            return inner

        lax.fori_loop(0, p, chunk_grads, 0)
        own[i, 0] = dk_acc[block(p), :] * scale
        own[i, 1] = dv_acc[block(p), :]

        @pl.when(step == pairs - 1)
        def _():
            for o in range(1, G):
                r1_wait(o)
            total = pacc[g]
            for o in range(1, G):
                total = total + pr1[peer(g, o, G)].astype(jnp.float32)
            pacc[g] = total
            ps2[...] = total.astype(jnp.bfloat16)
            for o in range(1, n):
                r2(o).start()

        @pl.when((lag > 0) & (step >= lag))
        def _():
            add_up(step - lag)

        return carry

    lax.fori_loop(0, pairs, one_pair, 0)

    def write_query_grad(r):
        parts = [dq_acc[r * H + h].T.reshape(L, F, E) for h in range(H)]
        dq_ref[:, r] = (jnp.concatenate(parts, axis=1) * scale).astype(jnp.bfloat16)

    def add_rest(k, carry):
        add_up(k)
        return carry

    left = jnp.maximum(pairs - lag, 0)

    for o in range(1, n):
        r2_wait(o)
    total = pacc[g, p]
    for o in range(1, n):
        total = total + pr2[peer(p, o, n)].astype(jnp.float32)
    pg_all[g] = total.astype(jnp.bfloat16)

    def r3(o):
        dest = peer(g, o, G)
        return remote(pg_all.at[g], pg_all.at[g], r3_send.at[dest], r3_recv.at[g], at(gg=dest))

    def r3_wait(o):
        src = peer(g, o, G)
        remote(pg_all.at[src], pg_all.at[src], r3_send.at[src], r3_recv.at[src], at(gg=src)).wait_recv()

    for o in range(1, G):
        r3(o).start()
    lax.fori_loop(left, jnp.where(p > 0, pairs, left), add_rest, 0)
    for r in range(R):
        write_query_grad(r)
    out_copy.start()
    for copy in weight_copies():
        copy.wait()
    for o in range(1, G):
        r3_wait(o)

    def project(tt):
        result = None
        for which in range(2):
            for h in range(H):
                low = pg_all[:, which, h].reshape(G * piece, E)
                term = dot_nt(low, weights[which, tt, :, h * E : (h + 1) * E])
                result = term if result is None else result + term
        return result

    def x_copy(o):
        dest = peer(t, o, T)
        return remote(xs.at[o - 1], xr.at[o - 1], x_send.at[o - 1], x_recv.at[o - 1], at(tt=dest))

    for o in range(1, T):
        xs[o - 1] = project(peer(t, o, T)).astype(jnp.bfloat16)
        x_copy(o).start()
    opart[...] = project(t)

    result = opart[...]
    for o in range(1, T):
        x_copy(o).wait_recv()
        result = result + xr[o - 1].astype(jnp.float32)
    og[g] = result.astype(jnp.bfloat16)

    def o_copy(o):
        dest = peer(g, o, G)
        return remote(og.at[g], og.at[g], o_send.at[dest], o_recv.at[g], at(gg=dest))

    def o_wait(o):
        src = peer(g, o, G)
        remote(og.at[src], og.at[src], o_send.at[src], o_recv.at[src], at(gg=src)).wait_recv()

    for o in range(1, G):
        o_copy(o).start()
    lax.fori_loop(left, jnp.where(p > 0, left, pairs), add_rest, 0)
    for which, ref in enumerate((dkey_ref, dvalue_ref)):
        for i in range(pairs):
            wide[which, pl.ds(i, L, stride=pairs), :] = own[i, which]
        ref[...] = wide[which, : L * pairs].astype(jnp.bfloat16)
    for o in range(1, G):
        o_wait(o)
    for gg in range(G):
        out_ref[:, gg * quarter : (gg + 1) * quarter] = og[gg]
    out_copy.wait()

    def pair_sent(i, carry):
        def chunk_sent(j, inner):
            chunk_copy(kv_ref.at[i], j, i).wait_send()
            return inner

        def grad_sent(j, inner):
            grad_copy(j, i).wait_send()
            return inner

        lax.fori_loop(0, jnp.where(p < n - 1, p + 1, 0), chunk_sent, 0)
        return lax.fori_loop(0, p, grad_sent, carry)

    lax.fori_loop(0, pairs, pair_sent, 0)
    for o in range(1, n):
        prompt_a(o).wait_send()
        r2(o).wait_send()
        for oo in range(1, G):
            prompt_b(o, oo).wait_send()
    for o in range(1, G):
        r1(o).wait_send()
        r3(o).wait_send()
        o_copy(o).wait_send()
    for o in range(1, T):
        x_copy(o).wait_send()


def hand_on(*refs):
    count = 4
    sources, targets, held = refs[:count], refs[count : 2 * count], refs[2 * count : 3 * count]
    in_sem, out_sem = refs[3 * count :]
    arriving = [pltpu.make_async_copy(sources[i], held[i], in_sem.at[i]) for i in range(count)]
    leaving = [pltpu.make_async_copy(held[i], targets[i], out_sem.at[i]) for i in range(count)]
    for copy in arriving:
        copy.start()
    for came, goes in zip(arriving, leaving):
        came.wait()
        goes.start()
    for copy in leaving:
        copy.wait()


def per_device(
    sizes,
    resp_query,
    response_key,
    response_value,
    resp_cotangent,
    prompt_key,
    prompt_value_rows,
    key_matrix,
    value_matrix,
    resp_lengths,
):
    n, G, T = sizes
    L, R, heads, E = resp_query.shape
    H = response_key.shape[2]
    pairs = R * H
    rows = L * heads // H
    prompt_rows = prompt_key.shape[0]
    piece = prompt_rows // G
    width = key_matrix.shape[0]
    quarter = width // T // G
    bf16, f32 = jnp.bfloat16, jnp.float32

    vmem = pl.BlockSpec(memory_space=pltpu.VMEM)
    anywhere = pl.BlockSpec(memory_space=pl.ANY)
    dma = pltpu.SemaphoreType.DMA
    scratch = [
        pltpu.VMEM((L, R, heads, E), bf16),
        pltpu.VMEM((L, R, heads, E), bf16),
        pltpu.VMEM((L, R, heads, E), bf16),
        pltpu.VMEM((2, max(L * pairs, prompt_rows * H), E), f32),
        pltpu.VMEM((pairs, 2, L, E), bf16),
        pltpu.VMEM((G, 2, H, piece, E), bf16),
        pltpu.VMEM((pairs, rows, E), bf16),
        pltpu.VMEM((pairs, rows, E), bf16),
        pltpu.VMEM((pairs, E, rows), bf16),
        pltpu.VMEM((pairs, E, rows), bf16),
        pltpu.VMEM((n, pairs, 2, L, E), bf16),
        pltpu.VMEM((n, G, 2, H, piece, E), bf16),
        pltpu.VMEM((n * (L + prompt_rows), E), bf16),
        pltpu.VMEM((n * (L + prompt_rows), E), bf16),
        pltpu.VMEM((E, n * (L + prompt_rows)), bf16),
        pltpu.VMEM((n * (L + prompt_rows), E), f32),
        pltpu.VMEM((n * (L + prompt_rows), E), f32),
        pltpu.VMEM((pairs, E, rows), f32),
        pltpu.VMEM((pairs, 2, L, E), f32),
        pltpu.VMEM((n, pairs, 2, L, E), bf16),
        pltpu.VMEM((n, pairs, 2, L, E), bf16),
        pltpu.VMEM((G, n, 2, H, piece, E), f32),
        pltpu.VMEM((G, n, 2, H, piece, E), bf16),
        pltpu.VMEM((G, n, 2, H, piece, E), bf16),
        pltpu.VMEM((n, 2, H, piece, E), bf16),
        pltpu.VMEM((n, 2, H, piece, E), bf16),
        pltpu.VMEM((G, 2, H, piece, E), bf16),
        pltpu.VMEM((2, T, quarter, H * E), bf16),
        pltpu.VMEM((prompt_rows, quarter), f32),
        pltpu.VMEM((max(T - 1, 1), prompt_rows, quarter), bf16),
        pltpu.VMEM((max(T - 1, 1), prompt_rows, quarter), bf16),
        pltpu.VMEM((G, prompt_rows, quarter), bf16),
        dma((2, T)),
        dma((3,)),
        dma((n, pairs)),
        dma((n, pairs)),
        dma((n,)),
        dma((n,)),
        dma((G, n)),
        dma((G, n)),
        dma((n, pairs)),
        dma((n, pairs)),
        dma((G,)),
        dma((G,)),
        dma((n,)),
        dma((n,)),
        dma((G,)),
        dma((G,)),
        dma((max(T - 1, 1),)),
        dma((max(T - 1, 1),)),
        dma((G,)),
        dma((G,)),
    ]
    results = pl.pallas_call(
        functools.partial(kernel, sizes),
        out_shape=(
            jax.ShapeDtypeStruct((L, R, heads, E), bf16),
            jax.ShapeDtypeStruct((L * pairs, E), bf16),
            jax.ShapeDtypeStruct((L * pairs, E), bf16),
            jax.ShapeDtypeStruct((prompt_rows, width // T), bf16),
        ),
        in_specs=[pl.BlockSpec(memory_space=pltpu.SMEM)] + [vmem] * 4 + [anywhere] * 4,
        out_specs=(anywhere, vmem, vmem, vmem),
        scratch_shapes=scratch,
        compiler_params=pltpu.CompilerParams(
            collective_id=0, has_side_effects=True, vmem_limit_bytes=60 * 1024 * 1024
        ),
    )(
        resp_lengths,
        response_key.reshape(L * pairs, E),
        response_value.reshape(L * pairs, E),
        prompt_key.reshape(prompt_rows * H, E),
        prompt_value_rows.reshape(prompt_rows * H, E),
        resp_query,
        resp_cotangent,
        key_matrix,
        value_matrix,
    )
    query_grad, key_grad, value_grad, out = pl.pallas_call(
        hand_on,
        out_shape=tuple(jax.ShapeDtypeStruct(x.shape, x.dtype) for x in results),
        in_specs=[anywhere] * 4,
        out_specs=(anywhere,) * 4,
        scratch_shapes=[pltpu.VMEM(x.shape, x.dtype) for x in results] + [dma((4,)), dma((4,))],
        compiler_params=pltpu.CompilerParams(vmem_limit_bytes=60 * 1024 * 1024),
    )(*results)
    shape = response_key.shape
    return (query_grad, key_grad.reshape(shape), value_grad.reshape(shape), out)


def solution(mesh):
    sizes = (mesh.shape["prefix"], mesh.shape["group"], mesh.shape["tensor"])
    placed = (
        P("prefix", "group", "tensor", None),
        P("prefix", "group", "tensor", None),
        P("prefix", "group", "tensor", None),
        P("prefix", "group", "tensor", None),
        P("prefix", "tensor", None),
        P("prefix", "tensor", None),
        P(None, "tensor"),
        P(None, "tensor"),
        P(),
    )
    return jax.shard_map(
        functools.partial(per_device, sizes),
        mesh=mesh,
        in_specs=placed,
        out_specs=(
            P("prefix", "group", "tensor", None),
            P("prefix", "group", "tensor", None),
            P("prefix", "group", "tensor", None),
            P("prefix", "tensor"),
        ),
        check_vma=False,
    )
```

```python
import functools
import math

import jax
import jax.numpy as jnp
from jax import lax
from jax.experimental import pallas as pl
from jax.experimental.pallas import tpu as pltpu
from jax.sharding import PartitionSpec as P

MESH = pl.DeviceIdType.MESH
masked_score = -1e30
log2_e = math.log2(math.e)


def dot_nt(a, b):
    return lax.dot_general(a, b, (((1,), (1,)), ((), ())), preferred_element_type=jnp.float32)


def dot_nn(a, b):
    return lax.dot_general(a, b, (((1,), (0,)), ((), ())), preferred_element_type=jnp.float32)


def kernel(
    sizes,
    len_ref,
    key_ref,
    value_ref,
    pkey_ref,
    pvalue_ref,
    q_hbm,
    cot_hbm,
    km_ref,
    vm_ref,
    dq_hbm,
    dkey_ref,
    dvalue_ref,
    out_ref,
    q_ref,
    cot_ref,
    dq_ref,
    wide,
    kv_ref,
    pr_ref,
    qs,
    cots,
    qts,
    cotts,
    kv_all,
    pr_all,
    s_buf,
    dp_buf,
    m_ref,
    l_ref,
    d_ref,
    dq_acc,
    own,
    gsend,
    grecv,
    pacc,
    ps1,
    pr1,
    ps2,
    pr2,
    pg_all,
    weights,
    opart,
    xs,
    xr,
    og,
    w_sem,
    q_sem,
    c_send,
    c_recv,
    a_send,
    a_recv,
    b_send,
    b_recv,
    g_send,
    g_recv,
    r1_send,
    r1_recv,
    r2_send,
    r2_recv,
    r3_send,
    r3_recv,
    x_send,
    x_recv,
    o_send,
    o_recv,
):
    n, G, T = sizes
    p = lax.axis_index("prefix")
    g = lax.axis_index("group")
    t = lax.axis_index("tensor")
    L, R, heads, E = q_ref.shape
    pairs = kv_ref.shape[0]
    H = pairs // R
    F = heads // H
    rows = L * F
    piece = pr_ref.shape[3]
    quarter = weights.shape[2]
    scale = 1.0 / math.sqrt(E)
    log_scale = scale * log2_e

    def at(pp=None, gg=None, tt=None):
        return (p if pp is None else pp, g if gg is None else gg, t if tt is None else tt)

    def peer(me, o, size):
        return lax.rem(me + o, size)

    def remote(src, dst, send, recv, where):
        return pltpu.make_async_remote_copy(
            src_ref=src, dst_ref=dst, send_sem=send, recv_sem=recv, device_id=where, device_id_type=MESH
        )

    barrier = pltpu.get_barrier_semaphore()
    for o in range(1, n):
        pl.semaphore_signal(barrier, inc=1, device_id=at(pp=peer(p, o, n)), device_id_type=MESH)
    for o in range(1, G):
        pl.semaphore_signal(barrier, inc=1, device_id=at(gg=peer(g, o, G)), device_id_type=MESH)
    for o in range(1, T):
        pl.semaphore_signal(barrier, inc=1, device_id=at(tt=peer(t, o, T)), device_id_type=MESH)

    half = quarter * G

    def weight_copies():
        copies = []
        for which, ref in enumerate((km_ref, vm_ref)):
            for tt in range(T):
                start = pl.multiple_of(tt * half + g * quarter, 16)
                copies.append(
                    pltpu.make_async_copy(
                        ref.at[pl.ds(start, quarter)], weights.at[which, tt], w_sem.at[which, tt]
                    )
                )
        return copies

    in_copies = (
        pltpu.make_async_copy(q_hbm, q_ref, q_sem.at[0]),
        pltpu.make_async_copy(cot_hbm, cot_ref, q_sem.at[1]),
    )
    out_copy = pltpu.make_async_copy(dq_ref, dq_hbm, q_sem.at[2])
    for copy in in_copies:
        copy.start()
    for copy in weight_copies():
        copy.start()

    for which, ref in enumerate((key_ref, value_ref)):
        wide[which, : L * pairs] = ref[...].astype(jnp.float32)
        for i in range(pairs):
            kv_ref[i, which] = wide[which, pl.ds(i, L, stride=pairs), :].astype(jnp.bfloat16)
    for which, ref in enumerate((pkey_ref, pvalue_ref)):
        wide[which, : G * piece * H] = ref[...].astype(jnp.float32)
        for gg in range(G):
            for h in range(H):
                rows_of = pl.ds(gg * piece * H + h, piece, stride=H)
                pr_ref[gg, which, h] = wide[which, rows_of, :].astype(jnp.bfloat16)

    pl.semaphore_wait(barrier, n + G + T - 3)

    def order(k):
        return lax.rem(k, R) * H + k // R

    up, down = lax.rem(p + 1, n), lax.rem(p + n - 1, n)

    def chunk_copy(src, j, i):
        return remote(src, kv_all.at[j, i], c_send.at[j, i], c_recv.at[j, i], at(pp=up))

    def chunk_wait(j, i):
        chunk_copy(kv_ref.at[i], j, i).wait_recv()

    def send_own(k):
        @pl.when((p < n - 1) & (k < pairs))
        def _():
            i = order(k)
            chunk_copy(kv_ref.at[i], p, i).start()

    def pass_on(k):
        @pl.when((p < n - 1) & (k < pairs))
        def _():
            i = order(k)

            def one(o, inner):
                chunk_wait(p - o, i)
                chunk_copy(kv_all.at[p - o, i], p - o, i).start()
                return inner

            lax.fori_loop(1, p + 1, one, 0)

    def prompt_a(o):
        dest = peer(p, o, n)
        return remote(pr_ref.at[g], pr_all.at[p, g], a_send.at[dest], a_recv.at[p], at(pp=dest))

    def prompt_a_wait(o):
        src = peer(p, o, n)
        remote(pr_ref.at[g], pr_all.at[src, g], a_send.at[src], a_recv.at[src], at(pp=src)).wait_recv()

    for o in range(1, n):
        prompt_a(o).start()

    send_own(0)
    send_own(1)

    def prompt_b(o, oo):
        src, dest = peer(p, o, n), peer(g, oo, G)
        return remote(
            pr_all.at[src, g], pr_all.at[src, g], b_send.at[dest, src], b_recv.at[g, src], at(gg=dest)
        )

    def prompt_b_wait(o, oo):
        src, frm = peer(p, o, n), peer(g, oo, G)
        remote(
            pr_all.at[src, frm], pr_all.at[src, frm], b_send.at[frm, src], b_recv.at[frm, src], at(gg=frm)
        ).wait_recv()

    pr_all[p] = pr_ref[...]
    pos = p * L + lax.broadcasted_iota(jnp.int32, (L, F, E), 0)
    for copy in in_copies:
        copy.wait()
    for r in range(R):
        length = len_ref[g * R + r]
        q = q_ref[:, r].astype(jnp.float32)
        c = cot_ref[:, r].astype(jnp.float32)
        for h in range(H):
            part = q[:, h * F : (h + 1) * F].reshape(rows, E)
            qs[r * H + h] = part.astype(jnp.bfloat16)
            qts[r * H + h] = part.T.astype(jnp.bfloat16)
            live = jnp.where(pos < length, c[:, h * F : (h + 1) * F], 0.0).reshape(rows, E)
            cots[r * H + h] = live.astype(jnp.bfloat16)
            cotts[r * H + h] = live.T.astype(jnp.bfloat16)
        if r == 0:
            for o in range(1, n):
                prompt_a_wait(o)
                for oo in range(1, G):
                    prompt_b(o, oo).start()
            pass_on(0)
            send_own(2)
    pass_on(1)
    send_own(3)
    for o in range(1, n):
        for oo in range(1, G):
            prompt_b_wait(o, oo)

    prompt_keys = n * G * piece

    def prompt_block(which, pair):
        return pr_all[:, :, which, lax.rem(pair, H)].reshape(prompt_keys, E)

    def block(j):
        return pl.ds(pl.multiple_of(j * L, L), L)

    prompt_rows = pl.ds(n * L, prompt_keys)

    def stats(pair, where, k, v, diag):
        s = dot_nn(k, qts[pair]) * log_scale
        if diag:
            key = lax.broadcasted_iota(jnp.int32, s.shape, 0)
            query = lax.broadcasted_iota(jnp.int32, s.shape, 1) // F
            s = jnp.where(key <= query, s, masked_score)
        dp = dot_nn(v, cotts[pair])
        s_buf[where, :] = s
        dp_buf[where, :] = dp
        top = jnp.max(s, axis=0, keepdims=True)
        if diag:
            e = jnp.exp2(s - top)
            l_ref[...] = jnp.sum(e, axis=0, keepdims=True)
            d_ref[...] = jnp.sum(e * dp, axis=0, keepdims=True)
            m_ref[...] = top
        else:
            m_old = m_ref[...]
            m_new = jnp.maximum(m_old, top)
            e = jnp.exp2(s - m_new)
            a = jnp.exp2(m_old - m_new)
            l_ref[...] = l_ref[...] * a + jnp.sum(e, axis=0, keepdims=True)
            d_ref[...] = d_ref[...] * a + jnp.sum(e * dp, axis=0, keepdims=True)
            m_ref[...] = m_new

    def grads(pair, where, k, first=False):
        prob = jnp.exp2(s_buf[where, :] - m_ref[...])
        ds = (prob * (dp_buf[where, :] - d_ref[...])).astype(jnp.bfloat16)
        dv = dot_nn(prob.astype(jnp.bfloat16), cots[pair])
        dk = dot_nn(ds, qs[pair]) * scale
        term = dot_nn(k.T, ds)
        if first:
            dq_acc[pair] = term
        else:
            dq_acc[pair] += term
        return dk, dv

    def grad_copy(j, i):
        return remote(gsend.at[j, i], grecv.at[j, i], g_send.at[j, i], g_recv.at[j, i], at(pp=down))

    def add_up(k):
        i = order(k)

        def one(j, inner):
            grad_copy(j, i).wait_recv()
            total = gsend[j, i].astype(jnp.float32) + grecv[j, i].astype(jnp.float32)
            gsend[j, i] = total.astype(jnp.bfloat16)
            grad_copy(j, i).start()
            return inner

        lax.fori_loop(0, p, one, 0)
        grad_copy(p, i).wait_recv()
        own[i] += grecv[p, i].astype(jnp.float32)

    lag = n - 1 - p

    def r1(o):
        dest = peer(g, o, G)
        return remote(ps1.at[dest], pr1.at[g], r1_send.at[dest], r1_recv.at[g], at(gg=dest))

    def r1_wait(o):
        src = peer(g, o, G)
        remote(ps1.at[src], pr1.at[src], r1_send.at[src], r1_recv.at[src], at(gg=src)).wait_recv()

    def r2(o):
        dest = peer(p, o, n)
        return remote(ps2.at[dest], pr2.at[p], r2_send.at[dest], r2_recv.at[p], at(pp=dest))

    def r2_wait(o):
        src = peer(p, o, n)
        remote(ps2.at[src], pr2.at[src], r2_send.at[src], r2_recv.at[src], at(pp=src)).wait_recv()

    pacc[...] = jnp.zeros_like(pacc)

    def one_pair(step, carry):
        i = order(step)

        pass_on(step + 2)
        send_own(step + 4)
        stats(i, block(p), kv_ref[i, 0], kv_ref[i, 1], True)
        stats(i, prompt_rows, prompt_block(0, i), prompt_block(1, i), False)

        def chunk_stats(o, inner):
            j = p - o

            @pl.when(p == n - 1)
            def _():
                chunk_wait(j, i)

            stats(i, block(j), kv_all[j, i, 0], kv_all[j, i, 1], False)
            return inner

        lax.fori_loop(1, p + 1, chunk_stats, 0)
        d_ref[...] = d_ref[...] / l_ref[...]
        m_ref[...] = m_ref[...] + jnp.log(l_ref[...]) * log2_e

        h = lax.rem(i, H)
        dk, dv = grads(i, prompt_rows, prompt_block(0, i), True)
        dk = dk.reshape(n, G, piece, E)
        dv = dv.reshape(n, G, piece, E)
        for gg in range(G):
            pacc[gg, :, 0, h] += dk[:, gg]
            pacc[gg, :, 1, h] += dv[:, gg]

        @pl.when(step == pairs - 1)
        def _():
            ps1[...] = pacc[...].astype(jnp.bfloat16)
            for o in range(1, G):
                r1(o).start()

        def chunk_grads(j, inner):
            dk, dv = grads(i, block(j), kv_all[j, i, 0])
            gsend[j, i, 0] = dk.astype(jnp.bfloat16)
            gsend[j, i, 1] = dv.astype(jnp.bfloat16)

            @pl.when(p == n - 1)
            def _():
                grad_copy(j, i).start()

            return inner

        lax.fori_loop(0, p, chunk_grads, 0)

        @pl.when(step == pairs - 1)
        def _():
            for o in range(1, G):
                r1_wait(o)
            total = pacc[g]
            for o in range(1, G):
                total = total + pr1[peer(g, o, G)].astype(jnp.float32)
            pacc[g] = total
            ps2[...] = total.astype(jnp.bfloat16)
            for o in range(1, n):
                r2(o).start()

        dk, dv = grads(i, block(p), kv_ref[i, 0])
        own[i, 0] = dk
        own[i, 1] = dv

        @pl.when((lag > 0) & (step >= lag))
        def _():
            add_up(step - lag)

        return carry

    lax.fori_loop(0, pairs, one_pair, 0)

    def write_query_grad(r):
        parts = [dq_acc[r * H + h].T.reshape(L, F, E) for h in range(H)]
        dq_ref[:, r] = (jnp.concatenate(parts, axis=1) * scale).astype(jnp.bfloat16)

    def add_rest(k, carry):
        add_up(k)
        return carry

    left = jnp.maximum(pairs - lag, 0)

    for o in range(1, n):
        r2_wait(o)
    total = pacc[g, p]
    for o in range(1, n):
        total = total + pr2[peer(p, o, n)].astype(jnp.float32)
    pg_all[g] = total.astype(jnp.bfloat16)

    def r3(o):
        dest = peer(g, o, G)
        return remote(pg_all.at[g], pg_all.at[g], r3_send.at[dest], r3_recv.at[g], at(gg=dest))

    def r3_wait(o):
        src = peer(g, o, G)
        remote(pg_all.at[src], pg_all.at[src], r3_send.at[src], r3_recv.at[src], at(gg=src)).wait_recv()

    for o in range(1, G):
        r3(o).start()
    lax.fori_loop(left, jnp.where(p >= n - 2, pairs, left), add_rest, 0)
    for r in range(R):
        write_query_grad(r)
    out_copy.start()
    for copy in weight_copies():
        copy.wait()
    for o in range(1, G):
        r3_wait(o)

    def project(tt):
        result = None
        for which in range(2):
            for h in range(H):
                low = pg_all[:, which, h].reshape(G * piece, E)
                term = dot_nt(low, weights[which, tt, :, h * E : (h + 1) * E])
                result = term if result is None else result + term
        return result

    def x_copy(o):
        dest = peer(t, o, T)
        return remote(xs.at[o - 1], xr.at[o - 1], x_send.at[o - 1], x_recv.at[o - 1], at(tt=dest))

    for o in range(1, T):
        xs[o - 1] = project(peer(t, o, T)).astype(jnp.bfloat16)
        x_copy(o).start()
    opart[...] = project(t)
    lax.fori_loop(left, jnp.where((p > 0) & (p < n - 2), pairs, left), add_rest, 0)

    result = opart[...]
    for o in range(1, T):
        x_copy(o).wait_recv()
        result = result + xr[o - 1].astype(jnp.float32)
    og[g] = result.astype(jnp.bfloat16)

    def o_copy(o):
        dest = peer(g, o, G)
        return remote(og.at[g], og.at[g], o_send.at[dest], o_recv.at[g], at(gg=dest))

    def o_wait(o):
        src = peer(g, o, G)
        remote(og.at[src], og.at[src], o_send.at[src], o_recv.at[src], at(gg=src)).wait_recv()

    for o in range(1, G):
        o_copy(o).start()
    lax.fori_loop(left, jnp.where((p > 0) | (n < 2), left, pairs), add_rest, 0)
    for which, ref in enumerate((dkey_ref, dvalue_ref)):
        for i in range(pairs):
            wide[which, pl.ds(i, L, stride=pairs), :] = own[i, which]
        ref[...] = wide[which, : L * pairs].astype(jnp.bfloat16)
    for o in range(1, G):
        o_wait(o)
    for gg in range(G):
        out_ref[:, gg * quarter : (gg + 1) * quarter] = og[gg]
    out_copy.wait()

    def pair_sent(i, carry):
        def chunk_sent(j, inner):
            chunk_copy(kv_ref.at[i], j, i).wait_send()
            return inner

        def grad_sent(j, inner):
            grad_copy(j, i).wait_send()
            return inner

        lax.fori_loop(0, jnp.where(p < n - 1, p + 1, 0), chunk_sent, 0)
        return lax.fori_loop(0, p, grad_sent, carry)

    lax.fori_loop(0, pairs, pair_sent, 0)
    for o in range(1, n):
        prompt_a(o).wait_send()
        r2(o).wait_send()
        for oo in range(1, G):
            prompt_b(o, oo).wait_send()
    for o in range(1, G):
        r1(o).wait_send()
        r3(o).wait_send()
        o_copy(o).wait_send()
    for o in range(1, T):
        x_copy(o).wait_send()


def hand_on(*refs):
    count = 4
    sources, targets, held = refs[:count], refs[count : 2 * count], refs[2 * count : 3 * count]
    in_sem, out_sem = refs[3 * count :]
    arriving = [pltpu.make_async_copy(sources[i], held[i], in_sem.at[i]) for i in range(count)]
    leaving = [pltpu.make_async_copy(held[i], targets[i], out_sem.at[i]) for i in range(count)]
    for copy in arriving:
        copy.start()
    for came, goes in zip(arriving, leaving):
        came.wait()
        goes.start()
    for copy in leaving:
        copy.wait()


def per_device(
    sizes,
    resp_query,
    response_key,
    response_value,
    resp_cotangent,
    prompt_key,
    prompt_value_rows,
    key_matrix,
    value_matrix,
    resp_lengths,
):
    n, G, T = sizes
    L, R, heads, E = resp_query.shape
    H = response_key.shape[2]
    pairs = R * H
    rows = L * heads // H
    prompt_rows = prompt_key.shape[0]
    piece = prompt_rows // G
    width = key_matrix.shape[0]
    quarter = width // T // G
    bf16, f32 = jnp.bfloat16, jnp.float32

    vmem = pl.BlockSpec(memory_space=pltpu.VMEM)
    anywhere = pl.BlockSpec(memory_space=pl.ANY)
    dma = pltpu.SemaphoreType.DMA
    scratch = [
        pltpu.VMEM((L, R, heads, E), bf16),
        pltpu.VMEM((L, R, heads, E), bf16),
        pltpu.VMEM((L, R, heads, E), bf16),
        pltpu.VMEM((2, max(L * pairs, prompt_rows * H), E), f32),
        pltpu.VMEM((pairs, 2, L, E), bf16),
        pltpu.VMEM((G, 2, H, piece, E), bf16),
        pltpu.VMEM((pairs, rows, E), bf16),
        pltpu.VMEM((pairs, rows, E), bf16),
        pltpu.VMEM((pairs, E, rows), bf16),
        pltpu.VMEM((pairs, E, rows), bf16),
        pltpu.VMEM((n, pairs, 2, L, E), bf16),
        pltpu.VMEM((n, G, 2, H, piece, E), bf16),
        pltpu.VMEM((n * L + n * prompt_rows, rows), f32),
        pltpu.VMEM((n * L + n * prompt_rows, rows), f32),
        pltpu.VMEM((1, rows), f32),
        pltpu.VMEM((1, rows), f32),
        pltpu.VMEM((1, rows), f32),
        pltpu.VMEM((pairs, E, rows), f32),
        pltpu.VMEM((pairs, 2, L, E), f32),
        pltpu.VMEM((n, pairs, 2, L, E), bf16),
        pltpu.VMEM((n, pairs, 2, L, E), bf16),
        pltpu.VMEM((G, n, 2, H, piece, E), f32),
        pltpu.VMEM((G, n, 2, H, piece, E), bf16),
        pltpu.VMEM((G, n, 2, H, piece, E), bf16),
        pltpu.VMEM((n, 2, H, piece, E), bf16),
        pltpu.VMEM((n, 2, H, piece, E), bf16),
        pltpu.VMEM((G, 2, H, piece, E), bf16),
        pltpu.VMEM((2, T, quarter, H * E), bf16),
        pltpu.VMEM((prompt_rows, quarter), f32),
        pltpu.VMEM((max(T - 1, 1), prompt_rows, quarter), bf16),
        pltpu.VMEM((max(T - 1, 1), prompt_rows, quarter), bf16),
        pltpu.VMEM((G, prompt_rows, quarter), bf16),
        dma((2, T)),
        dma((3,)),
        dma((n, pairs)),
        dma((n, pairs)),
        dma((n,)),
        dma((n,)),
        dma((G, n)),
        dma((G, n)),
        dma((n, pairs)),
        dma((n, pairs)),
        dma((G,)),
        dma((G,)),
        dma((n,)),
        dma((n,)),
        dma((G,)),
        dma((G,)),
        dma((max(T - 1, 1),)),
        dma((max(T - 1, 1),)),
        dma((G,)),
        dma((G,)),
    ]
    results = pl.pallas_call(
        functools.partial(kernel, sizes),
        out_shape=(
            jax.ShapeDtypeStruct((L, R, heads, E), bf16),
            jax.ShapeDtypeStruct((L * pairs, E), bf16),
            jax.ShapeDtypeStruct((L * pairs, E), bf16),
            jax.ShapeDtypeStruct((prompt_rows, width // T), bf16),
        ),
        in_specs=[pl.BlockSpec(memory_space=pltpu.SMEM)] + [vmem] * 4 + [anywhere] * 4,
        out_specs=(anywhere, vmem, vmem, vmem),
        scratch_shapes=scratch,
        compiler_params=pltpu.CompilerParams(
            collective_id=0, has_side_effects=True, vmem_limit_bytes=60 * 1024 * 1024
        ),
    )(
        resp_lengths,
        response_key.reshape(L * pairs, E),
        response_value.reshape(L * pairs, E),
        prompt_key.reshape(prompt_rows * H, E),
        prompt_value_rows.reshape(prompt_rows * H, E),
        resp_query,
        resp_cotangent,
        key_matrix,
        value_matrix,
    )
    query_grad, key_grad, value_grad, out = pl.pallas_call(
        hand_on,
        out_shape=tuple(jax.ShapeDtypeStruct(x.shape, x.dtype) for x in results),
        in_specs=[anywhere] * 4,
        out_specs=(anywhere,) * 4,
        scratch_shapes=[pltpu.VMEM(x.shape, x.dtype) for x in results] + [dma((4,)), dma((4,))],
        compiler_params=pltpu.CompilerParams(vmem_limit_bytes=60 * 1024 * 1024),
    )(*results)
    shape = response_key.shape
    return (query_grad, key_grad.reshape(shape), value_grad.reshape(shape), out)


def solution(mesh):
    sizes = (mesh.shape["prefix"], mesh.shape["group"], mesh.shape["tensor"])
    placed = (
        P("prefix", "group", "tensor", None),
        P("prefix", "group", "tensor", None),
        P("prefix", "group", "tensor", None),
        P("prefix", "group", "tensor", None),
        P("prefix", "tensor", None),
        P("prefix", "tensor", None),
        P(None, "tensor"),
        P(None, "tensor"),
        P(),
    )
    return jax.shard_map(
        functools.partial(per_device, sizes),
        mesh=mesh,
        in_specs=placed,
        out_specs=(
            P("prefix", "group", "tensor", None),
            P("prefix", "group", "tensor", None),
            P("prefix", "group", "tensor", None),
            P("prefix", "tensor"),
        ),
        check_vma=False,
    )
```

```python
import functools
import math

import jax
import jax.numpy as jnp
from jax import lax
from jax.experimental import pallas as pl
from jax.experimental.pallas import tpu as pltpu
from jax.sharding import PartitionSpec as P

MESH = pl.DeviceIdType.MESH
masked_score = -1e30
log2_e = math.log2(math.e)


def dot_nt(a, b):
    return lax.dot_general(a, b, (((1,), (1,)), ((), ())), preferred_element_type=jnp.float32)


def dot_nn(a, b):
    return lax.dot_general(a, b, (((1,), (0,)), ((), ())), preferred_element_type=jnp.float32)


def kernel(
    sizes,
    len_ref,
    key_ref,
    value_ref,
    pkey_ref,
    pvalue_ref,
    q_hbm,
    cot_hbm,
    km_ref,
    vm_ref,
    dq_hbm,
    dkey_ref,
    dvalue_ref,
    out_ref,
    q_ref,
    cot_ref,
    dq_ref,
    wide,
    kv_ref,
    pr_ref,
    qs,
    cots,
    qts,
    cotts,
    kv_all,
    pr_all,
    s_buf,
    dp_buf,
    m_ref,
    l_ref,
    d_ref,
    dq_acc,
    own,
    gsend,
    grecv,
    pacc,
    ps1,
    pr1,
    ps2,
    pr2,
    pg_all,
    weights,
    opart,
    xs,
    xr,
    og,
    w_sem,
    q_sem,
    c_send,
    c_recv,
    a_send,
    a_recv,
    b_send,
    b_recv,
    g_send,
    g_recv,
    r1_send,
    r1_recv,
    r2_send,
    r2_recv,
    r3_send,
    r3_recv,
    x_send,
    x_recv,
    o_send,
    o_recv,
):
    n, G, T = sizes
    p = lax.axis_index("prefix")
    g = lax.axis_index("group")
    t = lax.axis_index("tensor")
    L, R, heads, E = q_ref.shape
    pairs = kv_ref.shape[0]
    H = pairs // R
    F = heads // H
    rows = L * F
    piece = pr_ref.shape[3]
    quarter = weights.shape[2]
    scale = 1.0 / math.sqrt(E)
    log_scale = scale * log2_e

    def at(pp=None, gg=None, tt=None):
        return (p if pp is None else pp, g if gg is None else gg, t if tt is None else tt)

    def peer(me, o, size):
        return lax.rem(me + o, size)

    def remote(src, dst, send, recv, where):
        return pltpu.make_async_remote_copy(
            src_ref=src, dst_ref=dst, send_sem=send, recv_sem=recv, device_id=where, device_id_type=MESH
        )

    barrier = pltpu.get_barrier_semaphore()
    for o in range(1, n):
        pl.semaphore_signal(barrier, inc=1, device_id=at(pp=peer(p, o, n)), device_id_type=MESH)
    for o in range(1, G):
        pl.semaphore_signal(barrier, inc=1, device_id=at(gg=peer(g, o, G)), device_id_type=MESH)
    for o in range(1, T):
        pl.semaphore_signal(barrier, inc=1, device_id=at(tt=peer(t, o, T)), device_id_type=MESH)

    half = quarter * G

    def weight_copies():
        copies = []
        for which, ref in enumerate((km_ref, vm_ref)):
            for tt in range(T):
                start = pl.multiple_of(tt * half + g * quarter, 16)
                copies.append(
                    pltpu.make_async_copy(
                        ref.at[pl.ds(start, quarter)], weights.at[which, tt], w_sem.at[which, tt]
                    )
                )
        return copies

    in_copies = (
        pltpu.make_async_copy(q_hbm, q_ref, q_sem.at[0]),
        pltpu.make_async_copy(cot_hbm, cot_ref, q_sem.at[1]),
    )
    out_copy = pltpu.make_async_copy(dq_ref, dq_hbm, q_sem.at[2])
    for copy in in_copies:
        copy.start()
    for copy in weight_copies():
        copy.start()

    for which, ref in enumerate((key_ref, value_ref)):
        wide[which, : L * pairs] = ref[...].astype(jnp.float32)
        for i in range(pairs):
            kv_ref[i, which] = wide[which, pl.ds(i, L, stride=pairs), :].astype(jnp.bfloat16)
    for which, ref in enumerate((pkey_ref, pvalue_ref)):
        wide[which, : G * piece * H] = ref[...].astype(jnp.float32)
        for gg in range(G):
            for h in range(H):
                rows_of = pl.ds(gg * piece * H + h, piece, stride=H)
                pr_ref[gg, which, h] = wide[which, rows_of, :].astype(jnp.bfloat16)

    pl.semaphore_wait(barrier, n + G + T - 3)

    def order(k):
        return lax.rem(k, R) * H + k // R

    up, down = lax.rem(p + 1, n), lax.rem(p + n - 1, n)

    def chunk_copy(src, j, i):
        return remote(src, kv_all.at[j, i], c_send.at[j, i], c_recv.at[j, i], at(pp=up))

    def chunk_wait(j, i):
        chunk_copy(kv_ref.at[i], j, i).wait_recv()

    def send_own(k):
        @pl.when((p < n - 1) & (k < pairs))
        def _():
            i = order(k)
            chunk_copy(kv_ref.at[i], p, i).start()

    def pass_on(k):
        @pl.when((p < n - 1) & (k < pairs))
        def _():
            i = order(k)

            def one(o, inner):
                chunk_wait(p - o, i)
                chunk_copy(kv_all.at[p - o, i], p - o, i).start()
                return inner

            lax.fori_loop(1, p + 1, one, 0)

    def prompt_a(o):
        dest = peer(p, o, n)
        return remote(pr_ref.at[g], pr_all.at[p, g], a_send.at[dest], a_recv.at[p], at(pp=dest))

    def prompt_a_wait(o):
        src = peer(p, o, n)
        remote(pr_ref.at[g], pr_all.at[src, g], a_send.at[src], a_recv.at[src], at(pp=src)).wait_recv()

    for o in range(1, n):
        prompt_a(o).start()

    send_own(0)
    send_own(1)

    def prompt_b(o, oo):
        src, dest = peer(p, o, n), peer(g, oo, G)
        return remote(
            pr_all.at[src, g], pr_all.at[src, g], b_send.at[dest, src], b_recv.at[g, src], at(gg=dest)
        )

    def prompt_b_wait(o, oo):
        src, frm = peer(p, o, n), peer(g, oo, G)
        remote(
            pr_all.at[src, frm], pr_all.at[src, frm], b_send.at[frm, src], b_recv.at[frm, src], at(gg=frm)
        ).wait_recv()

    pr_all[p] = pr_ref[...]
    pos = p * L + lax.broadcasted_iota(jnp.int32, (L, F, E), 0)
    for copy in in_copies:
        copy.wait()
    for r in range(R):
        length = len_ref[g * R + r]
        q = q_ref[:, r].astype(jnp.float32)
        c = cot_ref[:, r].astype(jnp.float32)
        for h in range(H):
            part = q[:, h * F : (h + 1) * F].reshape(rows, E).astype(jnp.bfloat16)
            qs[r * H + h] = part
            qts[r * H + h] = part.T
            live = jnp.where(pos < length, c[:, h * F : (h + 1) * F], 0.0)
            live = live.reshape(rows, E).astype(jnp.bfloat16)
            cots[r * H + h] = live
            cotts[r * H + h] = live.T
        if r == 0:
            for o in range(1, n):
                prompt_a_wait(o)
                for oo in range(1, G):
                    prompt_b(o, oo).start()
            pass_on(0)
            send_own(2)
    pass_on(1)
    send_own(3)
    for o in range(1, n):
        for oo in range(1, G):
            prompt_b_wait(o, oo)

    prompt_keys = n * G * piece

    def prompt_block(which, pair):
        return pr_all[:, :, which, lax.rem(pair, H)].reshape(prompt_keys, E)

    def block(j):
        return pl.ds(pl.multiple_of(j * L, L), L)

    prompt_rows = pl.ds(n * L, prompt_keys)

    def stats(pair, where, k, v, diag):
        s = dot_nn(k, qts[pair]) * log_scale
        if diag:
            key = lax.broadcasted_iota(jnp.int32, s.shape, 0)
            query = lax.broadcasted_iota(jnp.int32, s.shape, 1) // F
            s = jnp.where(key <= query, s, masked_score)
        dp = dot_nn(v, cotts[pair])
        s_buf[where, :] = s
        dp_buf[where, :] = dp
        top = jnp.max(s, axis=0, keepdims=True)
        if diag:
            e = jnp.exp2(s - top)
            l_ref[...] = jnp.sum(e, axis=0, keepdims=True)
            d_ref[...] = jnp.sum(e * dp, axis=0, keepdims=True)
            m_ref[...] = top
        else:
            m_old = m_ref[...]
            m_new = jnp.maximum(m_old, top)
            e = jnp.exp2(s - m_new)
            a = jnp.exp2(m_old - m_new)
            l_ref[...] = l_ref[...] * a + jnp.sum(e, axis=0, keepdims=True)
            d_ref[...] = d_ref[...] * a + jnp.sum(e * dp, axis=0, keepdims=True)
            m_ref[...] = m_new

    def grads(pair, where, k, first=False):
        prob = jnp.exp2(s_buf[where, :] - m_ref[...])
        ds = (prob * (dp_buf[where, :] - d_ref[...])).astype(jnp.bfloat16)
        dv = dot_nn(prob.astype(jnp.bfloat16), cots[pair])
        dk = dot_nn(ds, qs[pair]) * scale
        term = dot_nn(k.T, ds)
        if first:
            dq_acc[pair] = term
        else:
            dq_acc[pair] += term
        return dk, dv

    def grad_copy(j, i):
        return remote(gsend.at[j, i], grecv.at[j, i], g_send.at[j, i], g_recv.at[j, i], at(pp=down))

    def add_up(k):
        i = order(k)

        def one(j, inner):
            grad_copy(j, i).wait_recv()
            total = gsend[j, i].astype(jnp.float32) + grecv[j, i].astype(jnp.float32)
            gsend[j, i] = total.astype(jnp.bfloat16)
            grad_copy(j, i).start()
            return inner

        lax.fori_loop(0, p, one, 0)
        grad_copy(p, i).wait_recv()
        own[i] += grecv[p, i].astype(jnp.float32)

    lag = n - 1 - p

    def r1(o):
        dest = peer(g, o, G)
        return remote(ps1.at[dest], pr1.at[g], r1_send.at[dest], r1_recv.at[g], at(gg=dest))

    def r1_wait(o):
        src = peer(g, o, G)
        remote(ps1.at[src], pr1.at[src], r1_send.at[src], r1_recv.at[src], at(gg=src)).wait_recv()

    def r2(o):
        dest = peer(p, o, n)
        return remote(ps2.at[dest], pr2.at[p], r2_send.at[dest], r2_recv.at[p], at(pp=dest))

    def r2_wait(o):
        src = peer(p, o, n)
        remote(ps2.at[src], pr2.at[src], r2_send.at[src], r2_recv.at[src], at(pp=src)).wait_recv()

    pacc[...] = jnp.zeros_like(pacc)

    def one_pair(step, carry):
        i = order(step)

        pass_on(step + 2)
        send_own(step + 4)
        stats(i, block(p), kv_ref[i, 0], kv_ref[i, 1], True)
        stats(i, prompt_rows, prompt_block(0, i), prompt_block(1, i), False)

        def chunk_stats(o, inner):
            j = p - o

            @pl.when(p == n - 1)
            def _():
                chunk_wait(j, i)

            stats(i, block(j), kv_all[j, i, 0], kv_all[j, i, 1], False)
            return inner

        lax.fori_loop(1, p + 1, chunk_stats, 0)
        d_ref[...] = d_ref[...] / l_ref[...]
        m_ref[...] = m_ref[...] + jnp.log(l_ref[...]) * log2_e

        h = lax.rem(i, H)
        dk, dv = grads(i, prompt_rows, prompt_block(0, i), True)
        dk = dk.reshape(n, G, piece, E)
        dv = dv.reshape(n, G, piece, E)
        for gg in range(G):
            pacc[gg, :, 0, h] += dk[:, gg]
            pacc[gg, :, 1, h] += dv[:, gg]

        @pl.when(step == pairs - 1)
        def _():
            ps1[...] = pacc[...].astype(jnp.bfloat16)
            for o in range(1, G):
                r1(o).start()

        def chunk_grads(j, inner):
            dk, dv = grads(i, block(j), kv_all[j, i, 0])
            gsend[j, i, 0] = dk.astype(jnp.bfloat16)
            gsend[j, i, 1] = dv.astype(jnp.bfloat16)

            @pl.when(p == n - 1)
            def _():
                grad_copy(j, i).start()

            return inner

        lax.fori_loop(0, p, chunk_grads, 0)

        @pl.when(step == pairs - 1)
        def _():
            for o in range(1, G):
                r1_wait(o)
            total = pacc[g]
            for o in range(1, G):
                total = total + pr1[peer(g, o, G)].astype(jnp.float32)
            pacc[g] = total
            ps2[...] = total.astype(jnp.bfloat16)
            for o in range(1, n):
                r2(o).start()

        dk, dv = grads(i, block(p), kv_ref[i, 0])
        own[i, 0] = dk
        own[i, 1] = dv

        @pl.when((lag > 0) & (step >= lag))
        def _():
            add_up(step - lag)

        return carry

    lax.fori_loop(0, pairs, one_pair, 0)

    def write_query_grad(r):
        parts = [dq_acc[r * H + h].T.reshape(L, F, E) for h in range(H)]
        dq_ref[:, r] = (jnp.concatenate(parts, axis=1) * scale).astype(jnp.bfloat16)

    def add_rest(k, carry):
        add_up(k)
        return carry

    left = jnp.maximum(pairs - lag, 0)

    write_query_grad(0)
    for o in range(1, n):
        r2_wait(o)
    total = pacc[g, p]
    for o in range(1, n):
        total = total + pr2[peer(p, o, n)].astype(jnp.float32)
    pg_all[g] = total.astype(jnp.bfloat16)

    def r3(o):
        dest = peer(g, o, G)
        return remote(pg_all.at[g], pg_all.at[g], r3_send.at[dest], r3_recv.at[g], at(gg=dest))

    def r3_wait(o):
        src = peer(g, o, G)
        remote(pg_all.at[src], pg_all.at[src], r3_send.at[src], r3_recv.at[src], at(gg=src)).wait_recv()

    for o in range(1, G):
        r3(o).start()
    lax.fori_loop(left, jnp.where(p >= n - 2, pairs, left), add_rest, 0)
    for r in range(1, R):
        write_query_grad(r)
    out_copy.start()
    for copy in weight_copies():
        copy.wait()
    for o in range(1, G):
        r3_wait(o)

    def project(tt):
        result = None
        for which in range(2):
            for h in range(H):
                low = pg_all[:, which, h].reshape(G * piece, E)
                term = dot_nt(low, weights[which, tt, :, h * E : (h + 1) * E])
                result = term if result is None else result + term
        return result

    def x_copy(o):
        dest = peer(t, o, T)
        return remote(xs.at[o - 1], xr.at[o - 1], x_send.at[o - 1], x_recv.at[o - 1], at(tt=dest))

    for o in range(1, T):
        xs[o - 1] = project(peer(t, o, T)).astype(jnp.bfloat16)
        x_copy(o).start()
    opart[...] = project(t)
    lax.fori_loop(left, jnp.where((p > 0) & (p < n - 2), pairs, left), add_rest, 0)

    result = opart[...]
    for o in range(1, T):
        x_copy(o).wait_recv()
        result = result + xr[o - 1].astype(jnp.float32)
    og[g] = result.astype(jnp.bfloat16)

    def o_copy(o):
        dest = peer(g, o, G)
        return remote(og.at[g], og.at[g], o_send.at[dest], o_recv.at[g], at(gg=dest))

    def o_wait(o):
        src = peer(g, o, G)
        remote(og.at[src], og.at[src], o_send.at[src], o_recv.at[src], at(gg=src)).wait_recv()

    for o in range(1, G):
        o_copy(o).start()
    lax.fori_loop(left, jnp.where((p > 0) | (n < 2), left, pairs), add_rest, 0)
    for which, ref in enumerate((dkey_ref, dvalue_ref)):
        for i in range(pairs):
            wide[which, pl.ds(i, L, stride=pairs), :] = own[i, which]
        ref[...] = wide[which, : L * pairs].astype(jnp.bfloat16)
    for o in range(1, G):
        o_wait(o)
    for gg in range(G):
        out_ref[:, gg * quarter : (gg + 1) * quarter] = og[gg]
    out_copy.wait()

    def pair_sent(i, carry):
        def chunk_sent(j, inner):
            chunk_copy(kv_ref.at[i], j, i).wait_send()
            return inner

        def grad_sent(j, inner):
            grad_copy(j, i).wait_send()
            return inner

        lax.fori_loop(0, jnp.where(p < n - 1, p + 1, 0), chunk_sent, 0)
        return lax.fori_loop(0, p, grad_sent, carry)

    lax.fori_loop(0, pairs, pair_sent, 0)
    for o in range(1, n):
        prompt_a(o).wait_send()
        r2(o).wait_send()
        for oo in range(1, G):
            prompt_b(o, oo).wait_send()
    for o in range(1, G):
        r1(o).wait_send()
        r3(o).wait_send()
        o_copy(o).wait_send()
    for o in range(1, T):
        x_copy(o).wait_send()


hand_parts = 4


def hand_on(*refs):
    count = 4
    sources, targets, held = refs[:count], refs[count : 2 * count], refs[2 * count : 3 * count]
    in_sem, out_sem = refs[3 * count :]
    arriving, leaving = [], []
    for i in range(count):
        part = sources[i].shape[0] // hand_parts
        for k in range(hand_parts):
            here = pl.ds(k * part, part)
            arriving.append(pltpu.make_async_copy(sources[i].at[here], held[i].at[here], in_sem.at[i, k]))
            leaving.append(pltpu.make_async_copy(held[i].at[here], targets[i].at[here], out_sem.at[i, k]))
    for copy in arriving:
        copy.start()
    for came, goes in zip(arriving, leaving):
        came.wait()
        goes.start()
    for copy in leaving:
        copy.wait()


def per_device(
    sizes,
    resp_query,
    response_key,
    response_value,
    resp_cotangent,
    prompt_key,
    prompt_value_rows,
    key_matrix,
    value_matrix,
    resp_lengths,
):
    n, G, T = sizes
    L, R, heads, E = resp_query.shape
    H = response_key.shape[2]
    pairs = R * H
    rows = L * heads // H
    prompt_rows = prompt_key.shape[0]
    piece = prompt_rows // G
    width = key_matrix.shape[0]
    quarter = width // T // G
    bf16, f32 = jnp.bfloat16, jnp.float32

    vmem = pl.BlockSpec(memory_space=pltpu.VMEM)
    anywhere = pl.BlockSpec(memory_space=pl.ANY)
    dma = pltpu.SemaphoreType.DMA
    scratch = [
        pltpu.VMEM((L, R, heads, E), bf16),
        pltpu.VMEM((L, R, heads, E), bf16),
        pltpu.VMEM((L, R, heads, E), bf16),
        pltpu.VMEM((2, max(L * pairs, prompt_rows * H), E), f32),
        pltpu.VMEM((pairs, 2, L, E), bf16),
        pltpu.VMEM((G, 2, H, piece, E), bf16),
        pltpu.VMEM((pairs, rows, E), bf16),
        pltpu.VMEM((pairs, rows, E), bf16),
        pltpu.VMEM((pairs, E, rows), bf16),
        pltpu.VMEM((pairs, E, rows), bf16),
        pltpu.VMEM((n, pairs, 2, L, E), bf16),
        pltpu.VMEM((n, G, 2, H, piece, E), bf16),
        pltpu.VMEM((n * L + n * prompt_rows, rows), f32),
        pltpu.VMEM((n * L + n * prompt_rows, rows), f32),
        pltpu.VMEM((1, rows), f32),
        pltpu.VMEM((1, rows), f32),
        pltpu.VMEM((1, rows), f32),
        pltpu.VMEM((pairs, E, rows), f32),
        pltpu.VMEM((pairs, 2, L, E), f32),
        pltpu.VMEM((n, pairs, 2, L, E), bf16),
        pltpu.VMEM((n, pairs, 2, L, E), bf16),
        pltpu.VMEM((G, n, 2, H, piece, E), f32),
        pltpu.VMEM((G, n, 2, H, piece, E), bf16),
        pltpu.VMEM((G, n, 2, H, piece, E), bf16),
        pltpu.VMEM((n, 2, H, piece, E), bf16),
        pltpu.VMEM((n, 2, H, piece, E), bf16),
        pltpu.VMEM((G, 2, H, piece, E), bf16),
        pltpu.VMEM((2, T, quarter, H * E), bf16),
        pltpu.VMEM((prompt_rows, quarter), f32),
        pltpu.VMEM((max(T - 1, 1), prompt_rows, quarter), bf16),
        pltpu.VMEM((max(T - 1, 1), prompt_rows, quarter), bf16),
        pltpu.VMEM((G, prompt_rows, quarter), bf16),
        dma((2, T)),
        dma((3,)),
        dma((n, pairs)),
        dma((n, pairs)),
        dma((n,)),
        dma((n,)),
        dma((G, n)),
        dma((G, n)),
        dma((n, pairs)),
        dma((n, pairs)),
        dma((G,)),
        dma((G,)),
        dma((n,)),
        dma((n,)),
        dma((G,)),
        dma((G,)),
        dma((max(T - 1, 1),)),
        dma((max(T - 1, 1),)),
        dma((G,)),
        dma((G,)),
    ]
    results = pl.pallas_call(
        functools.partial(kernel, sizes),
        out_shape=(
            jax.ShapeDtypeStruct((L, R, heads, E), bf16),
            jax.ShapeDtypeStruct((L * pairs, E), bf16),
            jax.ShapeDtypeStruct((L * pairs, E), bf16),
            jax.ShapeDtypeStruct((prompt_rows, width // T), bf16),
        ),
        in_specs=[pl.BlockSpec(memory_space=pltpu.SMEM)] + [vmem] * 4 + [anywhere] * 4,
        out_specs=(anywhere, vmem, vmem, vmem),
        scratch_shapes=scratch,
        compiler_params=pltpu.CompilerParams(
            collective_id=0, has_side_effects=True, vmem_limit_bytes=60 * 1024 * 1024
        ),
    )(
        resp_lengths,
        response_key.reshape(L * pairs, E),
        response_value.reshape(L * pairs, E),
        prompt_key.reshape(prompt_rows * H, E),
        prompt_value_rows.reshape(prompt_rows * H, E),
        resp_query,
        resp_cotangent,
        key_matrix,
        value_matrix,
    )
    query_grad, key_grad, value_grad, out = pl.pallas_call(
        hand_on,
        out_shape=tuple(jax.ShapeDtypeStruct(x.shape, x.dtype) for x in results),
        in_specs=[anywhere] * 4,
        out_specs=(anywhere,) * 4,
        scratch_shapes=[pltpu.VMEM(x.shape, x.dtype) for x in results] + [dma((4, hand_parts)), dma((4, hand_parts))],
        compiler_params=pltpu.CompilerParams(vmem_limit_bytes=60 * 1024 * 1024),
    )(*results)
    shape = response_key.shape
    return (query_grad, key_grad.reshape(shape), value_grad.reshape(shape), out)


def solution(mesh):
    sizes = (mesh.shape["prefix"], mesh.shape["group"], mesh.shape["tensor"])
    placed = (
        P("prefix", "group", "tensor", None),
        P("prefix", "group", "tensor", None),
        P("prefix", "group", "tensor", None),
        P("prefix", "group", "tensor", None),
        P("prefix", "tensor", None),
        P("prefix", "tensor", None),
        P(None, "tensor"),
        P(None, "tensor"),
        P(),
    )
    return jax.shard_map(
        functools.partial(per_device, sizes),
        mesh=mesh,
        in_specs=placed,
        out_specs=(
            P("prefix", "group", "tensor", None),
            P("prefix", "group", "tensor", None),
            P("prefix", "group", "tensor", None),
            P("prefix", "tensor"),
        ),
        check_vma=False,
    )
```
